32 devices in a mesh: rep: 2 (over y), seq: 4 (over z), sub: 4 (over x, core).
Axes of the slice: x: 2, y: 2, z: 4, core: 2. Of those that a mesh axis runs over, the one named last changes fastest.
Arguments:
- queries: bfloat16 [4096, 768], P(('rep', 'seq', 'sub')), parts along dimension 0, may hold values from -96 to 96
- keys: bfloat16 [4096, 768], P(('rep', 'seq', 'sub')), parts along dimension 0, may hold values from -7.2 to 7.2
- values: bfloat16 [4096, 768], P(('rep', 'seq', 'sub')), parts along dimension 0, may hold values from -24 to 24
- offsets: int32 [12], replicated, may hold values from 0 to 3
Outputs:
- attended: bfloat16 [4096, 768], P(('rep', 'seq', 'sub')), parts along dimension 0
The draws below stay inside these ranges and needn't reach their ends.
There are 2 independent parts, one for each index of `rep`. The reference program is written for one: setup_inputs(seed, part) draws one part's arguments, and reference() takes and returns one part's arrays. A program takes and returns all parts, laid end to end along the dimension named above; an argument that names none is the same for every part. Nothing has to cross between parts.
All inputs are finite; a program needn't handle non-finite values.
Results may differ from the reference program's by a relative error of at most 0.0041.
Values may be sent and summed in bfloat16 or wider, within the bound.
No kernel may reach another device: no remote copies, remote signals or barrier semaphores. Data moves between devices by JAX's collectives and lax.ppermute only.
A program may use at most 64 MiB of HBM per device.

```python
import jax
import jax.numpy as jnp
from jax import lax

ATTENTION_HEADS = 12
HEAD_DIMENSION = 64
WIDTH = 768
SEG0 = 512
DILATION_RATE = 4
TILE_TOKENS = 2048


def draw_queries(key, part):
    key = jax.random.fold_in(key, 5)
    result = 1.2 * jnp.clip(jax.random.normal(key, (TILE_TOKENS, ATTENTION_HEADS * HEAD_DIMENSION), jnp.float32), -6.0, 6.0)
    return result.astype(jnp.bfloat16)


def draw_keys(key, part):
    key = jax.random.fold_in(key, 3)
    result = 1.2 * jnp.clip(jax.random.normal(key, (TILE_TOKENS, ATTENTION_HEADS * HEAD_DIMENSION), jnp.float32), -6.0, 6.0)
    return result.astype(jnp.bfloat16)


def place_ends(values, key, low, top_value):
    place = [jax.random.randint(jax.random.fold_in(key, axis), (), 0, length) for axis, length in enumerate(values.shape)]
    main_axis = values.shape.index(max(values.shape))
    next_to = place[:main_axis] + [(place[main_axis] + 1) % values.shape[main_axis]] + place[main_axis + 1:]
    return values.at[tuple(place)].set(low).at[tuple(next_to)].set(top_value)


def block_levels(stream_key, dims, shards, smallest, high):
    def one(dim, shards_of):
        draws = jax.random.uniform(jax.random.fold_in(jax.random.fold_in(stream_key, 6), dim), (shards_of,), jnp.float32, smallest / len(shards), high / len(shards))
        return jnp.repeat(jnp.exp(draws), dims[dim] // shards_of).reshape((-1,) + (1,) * (len(dims) - dim - 1))

    gain = one(*shards[0])
    for cut in shards[1:]:
        gain = gain * one(*cut)
    return gain


def centred(own_key, extent, width, most, split=(), held_as=jnp.bfloat16):
    values = jax.random.normal(own_key, extent, jnp.float32) * width
    if len(split) > 0:
        values = block_levels(own_key, extent, split, -0.22, 0.18) * values
    return jnp.clip(values, min=-most, max=most).astype(held_as)


def setup_inputs(seed: int = 0, part: int = 0) -> dict:
    key_list = jax.random.split(jax.random.key(seed), 5)
    part_splits = jax.random.split(jax.random.fold_in(key_list[4], part), 5)
    queries = draw_queries(jax.random.fold_in(jax.random.fold_in(key_list[4], part), 71), part)
    keys = draw_keys(jax.random.fold_in(jax.random.fold_in(key_list[4], part), 71), part)
    values = centred(part_splits[2], (TILE_TOKENS, WIDTH), 4.0, 24.0, ((0, 16),))
    offsets = place_ends(jax.random.randint(key_list[3], (ATTENTION_HEADS,), 0, DILATION_RATE), jax.random.fold_in(key_list[3], 1), 0, DILATION_RATE - 1).astype(jnp.int32)
    return dict(queries=queries, keys=keys, values=values, offsets=offsets)


def level_stats(query_heads, key_heads, value_heads):
    scores = jnp.einsum('hnd,hsd->hns', query_heads.astype(jnp.float32), key_heads.astype(jnp.float32), precision=lax.Precision.HIGHEST) * (HEAD_DIMENSION ** -0.5)
    top_score = scores.max(-1)
    weights = jnp.exp(scores - top_score[..., None])
    rounded = lax.optimization_barrier(weights.astype(jnp.bfloat16)).astype(jnp.float32)
    summed = jnp.einsum('hns,hsd->hnd', rounded, value_heads.astype(jnp.float32), precision=lax.Precision.HIGHEST)
    return top_score, weights.sum(-1), summed


def merge_level_outputs(level_zero_max, level_zero_sum, level_zero_output, level_one_max, level_one_sum, level_one_output, offsets, dilation):
    heads, tok_rows = level_zero_max.shape
    residue = jnp.arange(tok_rows, dtype=jnp.int32) % dilation
    member = residue[None, :] == offsets[:, None]
    wide_max = jnp.repeat(level_one_max, dilation, axis=1)
    wide_sum = jnp.repeat(level_one_sum, dilation, axis=1)
    wide_out = jnp.repeat(level_one_output, dilation, axis=1)
    top_both = jnp.where(member, jnp.maximum(level_zero_max, wide_max), level_zero_max)
    keep_zero = jnp.exp(level_zero_max - top_both)
    keep_one = jnp.where(member, jnp.exp(jnp.where(member, wide_max - top_both, 0.0)), 0.0)
    total = level_zero_sum * keep_zero + wide_sum * keep_one
    merged_output = (level_zero_output * keep_zero[..., None] + wide_out * keep_one[..., None]) / total[..., None]
    return merged_output.transpose(1, 0, 2).reshape(tok_rows, heads * merged_output.shape[2])


def reference(queries, keys, values, offsets):
    segments = TILE_TOKENS // SEG0

    def by_segment(index):
        start = index * SEG0

        def slice_heads(source_tensor):
            block = lax.dynamic_slice_in_dim(source_tensor, start, SEG0, 0)
            return block.reshape(SEG0, ATTENTION_HEADS, HEAD_DIMENSION).transpose(1, 0, 2)

        return level_stats(slice_heads(queries), slice_heads(keys), slice_heads(values))

    level_zero_max, level_zero_sum, level_zero_output = lax.map(by_segment, jnp.arange(segments, dtype=jnp.int32))
    level_zero_max = level_zero_max.transpose(1, 0, 2).reshape(ATTENTION_HEADS, TILE_TOKENS)
    level_zero_sum = level_zero_sum.transpose(1, 0, 2).reshape(ATTENTION_HEADS, TILE_TOKENS)
    level_zero_output = level_zero_output.transpose(1, 0, 2, 3).reshape(ATTENTION_HEADS, TILE_TOKENS, HEAD_DIMENSION)
    selector_fn = (jnp.arange(DILATION_RATE, dtype=jnp.int32)[:, None] == offsets[None, :]).astype(jnp.float32)

    def dilated(source_tensor):
        reshaped_input = source_tensor.reshape(TILE_TOKENS // DILATION_RATE, DILATION_RATE, ATTENTION_HEADS, HEAD_DIMENSION).astype(jnp.float32)
        return jnp.einsum('rjhd,jh->hrd', reshaped_input, selector_fn, precision=lax.Precision.HIGHEST)

    level_one_max, level_one_sum, level_one_output = level_stats(dilated(queries), dilated(keys), dilated(values))
    merged_output = merge_level_outputs(level_zero_max, level_zero_sum, level_zero_output, level_one_max, level_one_sum, level_one_output, offsets, DILATION_RATE)
    return merged_output.astype(jnp.bfloat16)
```

```python
import functools

import jax
import jax.numpy as jnp
from jax import lax
from jax.experimental import pallas as pl
from jax.experimental.pallas import tpu as pltpu
from jax.sharding import PartitionSpec as P

ATTENTION_HEADS = 12
HEAD_DIMENSION = 64
PAIR = 2 * HEAD_DIMENSION
LOWEST = -1e30


def round_up(count, step):
    return -(-count // step) * step


class Sizes:
    def __init__(self, rows, dilation, sub):
        self.rows, self.dilation, self.sub = rows, dilation, sub
        self.kept = rows // dilation
        self.rest = rows - self.kept
        self.kept_pad = round_up(self.kept, 16)
        self.rest_pad = round_up(self.rest, 16)
        self.all_pad = self.kept_pad + self.rest_pad
        self.shift = dilation.bit_length() - 1
        self.kept_keys = sub * self.kept_pad
        self.keys = sub * self.all_pad
        self.padded = self.kept_pad != self.kept or self.rest_pad != self.rest


def target_rows(sizes, position, offset):
    residue = jnp.bitwise_and(position, sizes.dilation - 1)
    group = jnp.right_shift(position, sizes.shift)
    slab = jnp.bitwise_and(residue - offset + sizes.dilation, sizes.dilation - 1)
    return jnp.where(slab == 0, group, sizes.kept_pad + (slab - 1) * sizes.kept + group)


def order_rows(sizes, offset):
    shape = (sizes.all_pad, sizes.rows)
    place = lax.broadcasted_iota(jnp.int32, shape, 0)
    target = target_rows(sizes, lax.broadcasted_iota(jnp.int32, (1, sizes.rows), 1), offset)
    return jnp.where(place == target, 1.0, 0.0).astype(jnp.bfloat16)


def restore_rows(sizes, offset):
    shape = (sizes.rows, sizes.all_pad)
    place = lax.broadcasted_iota(jnp.int32, shape, 1)
    target = target_rows(sizes, lax.broadcasted_iota(jnp.int32, shape, 0), offset)
    return jnp.where(place == target, 1.0, 0.0).astype(jnp.bfloat16)


def first_head(shape):
    return lax.broadcasted_iota(jnp.int32, shape, 1) < HEAD_DIMENSION


def dot(a, b):
    return jnp.dot(a, b, preferred_element_type=jnp.float32)


def dot_rows(a, b):
    return lax.dot_general(a, b, (((1,), (1,)), ((), ())), preferred_element_type=jnp.float32)


def order_kernel(sizes, off_ref, q_ref, k_ref, v_ref, qs_ref, qd_ref, kvd_ref, kr_ref, vr_ref):
    width = q_ref.shape[1]
    kept = sizes.kept_pad
    scale = HEAD_DIMENSION ** (-0.5)
    for pair in range(width // PAIR):
        cols = slice(pair * PAIR, (pair + 1) * PAIR)
        chosen = jnp.concatenate(
            [order_rows(sizes, off_ref[2 * pair]), order_rows(sizes, off_ref[2 * pair + 1])], 0
        )
        joined = jnp.concatenate([q_ref[:, cols], k_ref[:, cols], v_ref[:, cols]], 1)
        both = dot(chosen, joined)
        lead, follow = both[: sizes.all_pad], both[sizes.all_pad :]
        mask = first_head((sizes.all_pad, PAIR))
        q = jnp.where(mask, lead[:, :PAIR], follow[:, :PAIR]) * scale
        k = jnp.where(mask, lead[:, PAIR : 2 * PAIR], follow[:, PAIR : 2 * PAIR])
        v = jnp.where(mask, lead[:, 2 * PAIR :], follow[:, 2 * PAIR :])
        q, k, v = (x.astype(jnp.bfloat16) for x in (q, k, v))
        qs_ref[:, cols] = q
        qd_ref[:, cols] = q[:kept]
        kvd_ref[:, cols] = k[:kept]
        kvd_ref[:, width + pair * PAIR : width + (pair + 1) * PAIR] = v[:kept]
        kr_ref[:, cols] = k[kept:]
        vr_ref[:, cols] = v[kept:]


def both_heads(q):
    mask = first_head(q.shape)
    zero = jnp.zeros_like(q)
    return jnp.concatenate([jnp.where(mask, q, zero), jnp.where(mask, zero, q)], 0)


def with_ones(v):
    return jnp.concatenate([v, jnp.ones_like(v)], 1)


def hide(col, step, used):
    return jnp.where(lax.rem(col + step, step) < used, 0.0, LOWEST)


def weigh(scores, top, v):
    weights = jnp.exp(scores - top).astype(jnp.bfloat16)
    return dot(weights, with_ones(v))


def partial_kernel(sizes, others, *refs):
    q_refs, kv_refs, out_refs = refs[:others], refs[others : others + sizes.sub], refs[others + sizes.sub :]
    width = q_refs[0].shape[1]
    kept = sizes.kept_pad
    rows = others * kept
    lane = lax.broadcasted_iota(jnp.int32, (rows, PAIR), 1)
    stats = jnp.zeros((rows, PAIR), jnp.float32)
    for pair in range(width // PAIR):
        cols = slice(pair * PAIR, (pair + 1) * PAIR)
        vcols = slice(width + pair * PAIR, width + (pair + 1) * PAIR)
        q = jnp.concatenate([r[:, cols] for r in q_refs], 0)
        k = jnp.concatenate([r[:, cols] for r in kv_refs], 0)
        v = jnp.concatenate([r[:, vcols] for r in kv_refs], 0)
        scores = dot_rows(both_heads(q), k)
        if sizes.padded:
            scores += hide(lax.broadcasted_iota(jnp.int32, (1, sizes.kept_keys), 1), kept, sizes.kept)
        top = jnp.max(scores, 1, keepdims=True).astype(jnp.bfloat16).astype(jnp.float32)
        both = weigh(scores, top, v)
        lead, follow = both[:rows], both[rows:]
        out = jnp.where(first_head((rows, PAIR)), lead[:, :PAIR], follow[:, :PAIR]).astype(jnp.bfloat16)
        for n, r in enumerate(out_refs):
            r[:, cols] = out[n * kept : (n + 1) * kept]
        for n, part in enumerate((lead, follow)):
            head = 3 * (2 * pair + n)
            total = part[:, PAIR:]
            coarse = total.astype(jnp.bfloat16).astype(jnp.float32)
            stats = jnp.where(lane == head, top[n * rows : (n + 1) * rows], stats)
            stats = jnp.where(lane == head + 1, coarse, stats)
            stats = jnp.where(lane == head + 2, total - coarse, stats)
    stats = stats.astype(jnp.bfloat16)
    for n, r in enumerate(out_refs):
        r[:, width:] = stats[n * kept : (n + 1) * kept]


def final_kernel(sizes, others, *refs):
    off_ref, q_ref = refs[:2]
    kv_refs, kr_refs, vr_refs = (refs[2 + n * sizes.sub : 2 + (n + 1) * sizes.sub] for n in range(3))
    part_refs = refs[2 + 3 * sizes.sub : 2 + 3 * sizes.sub + others]
    out_ref = refs[-1]
    width = q_ref.shape[1]
    kept, rows = sizes.kept_pad, sizes.all_pad
    stats = [r[:, width:].astype(jnp.float32) for r in part_refs]
    for pair in range(width // PAIR):
        cols = slice(pair * PAIR, (pair + 1) * PAIR)
        vcols = slice(width + pair * PAIR, width + (pair + 1) * PAIR)
        k = jnp.concatenate([r[:, cols] for r in kv_refs] + [r[:, cols] for r in kr_refs], 0)
        v = jnp.concatenate([r[:, vcols] for r in kv_refs] + [r[:, cols] for r in vr_refs], 0)
        scores = dot_rows(both_heads(q_ref[:, cols]), k)
        if sizes.padded:
            col = lax.broadcasted_iota(jnp.int32, (1, sizes.keys), 1)
            here = hide(col, kept, sizes.kept)
            there = hide(col - sizes.kept_keys, sizes.rest_pad, sizes.rest)
            scores += jnp.where(col < sizes.kept_keys, here, there)
        top = jnp.max(scores, 1, keepdims=True)
        weights = jnp.exp(scores - top)
        twice = [weights[n * rows : n * rows + kept, : sizes.kept_keys] for n in range(2)]
        rest = [weights[n * rows : n * rows + kept, sizes.kept_keys :] for n in range(2)]
        weights = jnp.concatenate(
            [
                jnp.concatenate([twice[0] * 2.0, rest[0]], 1),
                weights[kept:rows],
                jnp.concatenate([twice[1] * 2.0, rest[1]], 1),
                weights[rows + kept :],
            ],
            0,
        )
        both = dot(weights.astype(jnp.bfloat16), with_ones(v))
        done = []
        for n in range(2):
            part = both[n * rows : (n + 1) * rows]
            out, total = part[:, :PAIR], part[:, PAIR:]
            head = 3 * (2 * pair + n)
            own_top = top[n * rows : n * rows + kept]
            tops = [s[:, head : head + 1] for s in stats]
            best = functools.reduce(jnp.maximum, tops, own_top)
            factor = jnp.exp(own_top - best)
            kept_out, kept_total = out[:kept] * factor, total[:kept] * factor
            for s, t, r in zip(stats, tops, part_refs):
                factor = jnp.exp(t - best)
                kept_out += r[:, cols].astype(jnp.float32) * factor
                kept_total += (s[:, head + 1 : head + 2] + s[:, head + 2 : head + 3]) * factor
            done.append(
                jnp.concatenate([kept_out / kept_total, out[kept:] / total[kept:]], 0)
            )
        result = jnp.where(first_head((rows, PAIR)), done[0], done[1]).astype(jnp.bfloat16)
        back = jnp.concatenate(
            [restore_rows(sizes, off_ref[2 * pair]), restore_rows(sizes, off_ref[2 * pair + 1])], 0
        )
        back = dot(back, result)
        out_ref[:, cols] = jnp.where(
            first_head((sizes.rows, PAIR)), back[: sizes.rows], back[sizes.rows :]
        ).astype(jnp.bfloat16)


def call(kernel, out_shape, operands, flops):
    vmem = pl.BlockSpec(memory_space=pltpu.VMEM)
    smem = pl.BlockSpec(memory_space=pltpu.SMEM)
    in_specs = [smem if x.dtype == jnp.int32 else vmem for x in operands]
    out_specs = jax.tree.map(lambda _: vmem, out_shape)
    size = sum(x.size * 2 for x in operands)
    return pl.pallas_call(
        kernel,
        out_shape=out_shape,
        in_specs=in_specs,
        out_specs=out_specs,
        cost_estimate=pl.CostEstimate(flops=flops, bytes_accessed=size, transcendentals=0),
        compiler_params=pltpu.CompilerParams(vmem_limit_bytes=32 * 1024 * 1024),
    )(*operands)


def per_device(queries, keys, values, offsets):
    rows, width = queries.shape
    seq, sub = lax.axis_size("seq"), lax.axis_size("sub")
    sizes = Sizes(rows, seq, sub)

    def array(count, columns=width):
        return jax.ShapeDtypeStruct((count, columns), jnp.bfloat16)

    def swap(x, axis, mask):
        return lax.ppermute(x, axis, [(n, n ^ mask) for n in range(lax.axis_size(axis))])

    q, q_kept, kv_kept, k_rest, v_rest = call(
        functools.partial(order_kernel, sizes),
        (
            array(sizes.all_pad),
            array(sizes.kept_pad),
            array(sizes.kept_pad, 2 * width),
            array(sizes.rest_pad),
            array(sizes.rest_pad),
        ),
        (offsets, queries, keys, values),
        2 * 10**7,
    )

    def gather(x):
        mine = [x] + [swap(x, "sub", mask) for mask in range(2, sub, 2)]
        return mine + [swap(y, "sub", 1) for y in mine]

    kv_kept, k_rest, v_rest = gather(kv_kept), gather(k_rest), gather(v_rest)
    masks = range(1, seq)
    visitors = [swap(q_kept, "seq", mask) for mask in masks]
    parts = call(
        functools.partial(partial_kernel, sizes, len(masks)),
        [array(sizes.kept_pad, width + PAIR)] * len(masks),
        (*visitors, *kv_kept),
        5 * 10**7,
    )
    parts = [swap(part, "seq", mask) for mask, part in zip(masks, parts)]
    return call(
        functools.partial(final_kernel, sizes, len(masks)),
        array(rows),
        (offsets, q, *kv_kept, *k_rest, *v_rest, *parts),
        20 * 10**7,
    )


def solution(mesh):
    placed = P(("rep", "seq", "sub"), None)
    return jax.shard_map(
        per_device,
        mesh=mesh,
        in_specs=(placed, placed, placed, P()),
        out_specs=placed,
        check_vma=False,
    )
```

```python
import functools

import jax
import jax.numpy as jnp
from jax import lax
from jax.experimental import pallas as pl
from jax.experimental.pallas import tpu as pltpu
from jax.sharding import PartitionSpec as P

ATTENTION_HEADS = 12
HEAD_DIMENSION = 64
PAIR = 2 * HEAD_DIMENSION
LOWEST = -1e30
LIMIT = 56
LEAD = 32
COST = (10**6, 10**6, 10**6, 10**6, 10**10, 10**6)


def round_up(count, step):
    return -(-count // step) * step


class Sizes:
    def __init__(self, rows, dilation, sub):
        self.rows, self.dilation, self.sub = rows, dilation, sub
        self.kept = rows // dilation
        self.rest = rows - self.kept
        self.kept_pad = round_up(self.kept, 16)
        self.rest_pad = round_up(self.rest, 16)
        self.all_pad = self.kept_pad + self.rest_pad
        self.first = 2 * self.kept_pad + LEAD * rows // 128
        self.second = 2 * self.all_pad - self.first
        self.shift = dilation.bit_length() - 1
        self.kept_keys = sub * self.kept_pad
        self.keys = sub * self.all_pad
        self.padded = self.kept_pad != self.kept or self.rest_pad != self.rest


def target_rows(sizes, position, offset):
    residue = jnp.bitwise_and(position, sizes.dilation - 1)
    group = jnp.right_shift(position, sizes.shift)
    slab = jnp.bitwise_and(residue - offset + sizes.dilation, sizes.dilation - 1)
    return jnp.where(slab == 0, group, sizes.kept_pad + (slab - 1) * sizes.kept + group)


def order_rows(sizes, offset):
    shape = (sizes.all_pad, sizes.rows)
    place = lax.broadcasted_iota(jnp.int32, shape, 0)
    target = target_rows(sizes, lax.broadcasted_iota(jnp.int32, (1, sizes.rows), 1), offset)
    return jnp.where(place == target, 1.0, 0.0).astype(jnp.bfloat16)


def restore_rows(sizes, offset):
    shape = (sizes.rows, sizes.all_pad)
    place = lax.broadcasted_iota(jnp.int32, shape, 1)
    target = target_rows(sizes, lax.broadcasted_iota(jnp.int32, shape, 0), offset)
    return jnp.where(place == target, 1.0, 0.0).astype(jnp.bfloat16)


def first_head(shape):
    return lax.broadcasted_iota(jnp.int32, shape, 1) < HEAD_DIMENSION


def dot(a, b):
    return jnp.dot(a, b, preferred_element_type=jnp.float32)


def dot_rows(a, b):
    return lax.dot_general(a, b, (((1,), (1,)), ((), ())), preferred_element_type=jnp.float32)


def select(both, rows, columns=slice(0, PAIR)):
    return jnp.where(first_head((rows, PAIR)), both[:rows, columns], both[rows:, columns])


def order_rows_of_pair(sizes, offset, pair, count):
    return jnp.concatenate([order_rows(sizes, offset(2 * pair + n))[:count] for n in range(2)], 0)


def fetch(sources, targets, sems):
    copies = [pltpu.make_async_copy(s, t, sems.at[n]) for n, (s, t) in enumerate(zip(sources, targets))]
    for copy in copies:
        copy.start()
    for copy in copies:
        copy.wait()


def first_kernel(sizes, *refs):
    qd_ref, first_ref, lanes_ref = refs[4:7]
    off_ref, q_ref, k_ref, v_ref, sems = refs[7:]
    fetch(refs[:4], (off_ref, q_ref, k_ref, v_ref), sems)
    kept = sizes.kept_pad
    count = sizes.first - kept
    scale = HEAD_DIMENSION ** (-0.5)
    lanes = lax.broadcasted_iota(jnp.int32, lanes_ref.shape, 0)
    spread_out = jnp.zeros(lanes_ref.shape, jnp.int32)
    for head in range(q_ref.shape[1] // HEAD_DIMENSION):
        spread_out = jnp.where(lanes == head, off_ref[head], spread_out)
    lanes_ref[...] = spread_out
    for pair in range(q_ref.shape[1] // PAIR):
        cols = slice(pair * PAIR, (pair + 1) * PAIR)
        chosen = order_rows_of_pair(sizes, lambda head: off_ref[head], pair, count)
        both = dot(chosen, jnp.concatenate([q_ref[:, cols], k_ref[:, cols], v_ref[:, cols]], 1))
        k = select(both, count, slice(PAIR, 2 * PAIR)).astype(jnp.bfloat16)
        qd_ref[:, cols] = (select(both, count)[:kept] * scale).astype(jnp.bfloat16)
        first_ref[:kept, cols] = k[:kept]
        first_ref[kept : 2 * kept, cols] = select(both, count, slice(2 * PAIR, 3 * PAIR))[:kept].astype(jnp.bfloat16)
        first_ref[2 * kept :, cols] = k[kept:]


def order_kernel(sizes, off_ref, q_ref, k_ref, v_ref, qs_ref, own_ref, second_ref):
    kept, count = sizes.kept_pad, sizes.all_pad
    scale = HEAD_DIMENSION ** (-0.5)
    for pair in range(q_ref.shape[1] // PAIR):
        cols = slice(pair * PAIR, (pair + 1) * PAIR)
        chosen = order_rows_of_pair(sizes, lambda head: off_ref[head], pair, count)
        both = dot(chosen, jnp.concatenate([q_ref[:, cols], k_ref[:, cols], v_ref[:, cols]], 1))
        qs_ref[:, cols] = (select(both, count) * scale).astype(jnp.bfloat16)
        k = select(both, count, slice(PAIR, 2 * PAIR)).astype(jnp.bfloat16)
        v = select(both, count, slice(2 * PAIR, 3 * PAIR)).astype(jnp.bfloat16)
        own = jnp.concatenate([k[:kept], v[:kept], k[kept:], v[kept:]], 0)
        own_ref[:, cols] = own
        second_ref[:, cols] = own[sizes.first :]


def rows_of(device, begin, count, cols):
    found = []
    for ref, base, size in device:
        low, high = max(begin, 0), min(begin + count, size)
        if low < high:
            found.append(ref[base + low : base + high, cols])
        begin -= size
    return found


def both_heads(q):
    mask = first_head(q.shape)
    zero = jnp.zeros_like(q)
    return jnp.concatenate([jnp.where(mask, q, zero), jnp.where(mask, zero, q)], 0)


def with_ones(v):
    return jnp.concatenate([v, jnp.ones_like(v)], 1)


def hide(col, step, used):
    return jnp.where(lax.rem(col + step, step) < used, 0.0, LOWEST)


def weigh(scores, top, v):
    weights = jnp.exp(scores - top).astype(jnp.bfloat16)
    return dot(weights, with_ones(v))


def sources(refs, parts):
    found = [[(r, 0, r.shape[0])] for r in refs[:2]]
    for n in range(2, len(refs), parts):
        for core in range(2):
            sizes = [(r, r.shape[0] // 2) for r in refs[n : n + parts]]
            found.append([(r, core * size, size) for r, size in sizes])
    return found


def join(devices, begin, count, cols):
    return [x for d in devices for x in rows_of(d, begin, count, cols)]


def collect_kernel(count, *refs):
    for n, r in enumerate(refs[:count]):
        refs[-1][n * r.shape[0] : (n + 1) * r.shape[0]] = r[...]


def partial_kernel(sizes, others, q_ref, *refs):
    out_refs = refs[-others:]
    devices = sources(refs[:-others], 1)
    width = q_ref.shape[1]
    kept = sizes.kept_pad
    rows = others * kept
    lane = lax.broadcasted_iota(jnp.int32, (rows, PAIR), 1)
    stats = jnp.zeros((rows, PAIR), jnp.float32)
    for pair in range(width // PAIR):
        cols = slice(pair * PAIR, (pair + 1) * PAIR)
        q = q_ref[:, cols]
        k = jnp.concatenate(join(devices, 0, kept, cols), 0)
        v = jnp.concatenate(join(devices, kept, kept, cols), 0)
        scores = dot_rows(both_heads(q), k)
        if sizes.padded:
            scores += hide(lax.broadcasted_iota(jnp.int32, (1, sizes.kept_keys), 1), kept, sizes.kept)
        top = jnp.max(scores, 1, keepdims=True).astype(jnp.bfloat16).astype(jnp.float32)
        both = weigh(scores, top, v)
        lead, follow = both[:rows], both[rows:]
        out = select(both, rows).astype(jnp.bfloat16)
        for n, r in enumerate(out_refs):
            r[:, cols] = out[n * kept : (n + 1) * kept]
        for n, part in enumerate((lead, follow)):
            head = 3 * (2 * pair + n)
            total = part[:, PAIR:]
            coarse = total.astype(jnp.bfloat16).astype(jnp.float32)
            stats = jnp.where(lane == head, top[n * rows : (n + 1) * rows], stats)
            stats = jnp.where(lane == head + 1, coarse, stats)
            stats = jnp.where(lane == head + 2, total - coarse, stats)
    stats = stats.astype(jnp.bfloat16)
    for n, r in enumerate(out_refs):
        r[:, width:] = stats[n * kept : (n + 1) * kept]


def dense_kernel(sizes, *refs):
    off_ref, q_ref = refs[:2]
    devices = sources(refs[2:-4], 2)
    out_ref, total_ref, top_ref, back_ref = refs[-4:]
    width = q_ref.shape[1]
    kept, rest, rows = sizes.kept_pad, sizes.rest_pad, sizes.all_pad
    begin = sizes.kept_keys
    for pair in range(width // PAIR):
        cols = slice(pair * PAIR, (pair + 1) * PAIR)
        k = jnp.concatenate(join(devices, 0, kept, cols) + join(devices, 2 * kept, rest, cols), 0)
        v = jnp.concatenate(join(devices, kept, kept, cols) + join(devices, kept + rows, rest, cols), 0)
        scores = dot_rows(both_heads(q_ref[:, cols]), k)
        if sizes.padded:
            col = lax.broadcasted_iota(jnp.int32, (1, sizes.keys), 1)
            here = hide(col, kept, sizes.kept)
            there = hide(col - begin + sizes.keys * rest, rest, sizes.rest)
            scores += jnp.where(col < begin, here, there)
        top = jnp.max(scores, 1, keepdims=True)
        weights = jnp.exp(scores - top)
        near, far = weights[:, :begin], weights[:, begin:]
        near = jnp.concatenate(
            [near[:kept] * 2.0, near[kept:rows], near[rows : rows + kept] * 2.0, near[rows + kept :]], 0
        )
        weights = jnp.concatenate([near, far], 1).astype(jnp.bfloat16)
        both = dot(weights, with_ones(v))
        out_ref[:, cols] = select(both, rows)
        total_ref[:, cols] = select(both, rows, slice(PAIR, 2 * PAIR))
        top_ref[:, cols] = jnp.where(first_head((kept, PAIR)), top[:kept], top[rows : rows + kept])
        for n in range(2):
            place = 2 * pair + n
            back_ref[place * sizes.rows : (place + 1) * sizes.rows] = restore_rows(sizes, off_ref[place : place + 1, 0:1])


def spread(width, lanes):
    lane = lax.broadcasted_iota(jnp.int32, (PAIR, width), 0)
    head = jnp.right_shift(lax.broadcasted_iota(jnp.int32, (PAIR, width), 1), HEAD_DIMENSION.bit_length() - 1)
    hits = [jnp.where(lane == 3 * head + n, 1.0, 0.0) for n in lanes]
    return sum(hits).astype(jnp.bfloat16)


def merge_kernel(sizes, *refs):
    out_ref, total_ref, top_ref, back_ref = refs[:4]
    part_refs, done_ref = refs[4:-1], refs[-1]
    others = len(part_refs)
    width = out_ref.shape[1]
    kept = sizes.kept_pad
    stats = jnp.concatenate([r[:, width:] for r in part_refs], 0)
    tops = dot(stats, spread(width, (0,)))
    totals = dot(stats, spread(width, (1, 2)))
    results = []
    for pair in range(width // PAIR):
        cols = slice(pair * PAIR, (pair + 1) * PAIR)
        out, total = out_ref[:, cols], total_ref[:, cols]
        top = top_ref[:, cols]
        theirs = [tops[n * kept : (n + 1) * kept, cols] for n in range(others)]
        best = functools.reduce(jnp.maximum, theirs, top)
        factor = jnp.exp(top - best)
        kept_out, kept_total = out[:kept] * factor, total[:kept] * factor
        for n, r in enumerate(part_refs):
            factor = jnp.exp(theirs[n] - best)
            kept_out += r[:, cols].astype(jnp.float32) * factor
            kept_total += totals[n * kept : (n + 1) * kept, cols] * factor
        result = jnp.concatenate([kept_out / kept_total, out[kept:] / total[kept:]], 0)
        results.append(result.astype(jnp.bfloat16))
    for pair, result in enumerate(results):
        cols = slice(pair * PAIR, (pair + 1) * PAIR)
        back = dot(back_ref[2 * sizes.rows * pair : 2 * sizes.rows * (pair + 1)], result)
        done_ref[:, cols] = select(back, sizes.rows).astype(jnp.bfloat16)


def call(kernel, out_shape, operands, flops, place=pltpu.VMEM, scratch=(), limit=24):
    spec = pl.BlockSpec(memory_space=place)
    smem = pl.BlockSpec(memory_space=pltpu.SMEM)
    in_specs = [smem if x.ndim == 1 and place == pltpu.VMEM else spec for x in operands]
    out_specs = jax.tree.map(lambda _: pl.BlockSpec(memory_space=pltpu.VMEM), out_shape)
    size = sum(x.size * 2 for x in operands)
    return pl.pallas_call(
        kernel,
        out_shape=out_shape,
        in_specs=in_specs,
        out_specs=out_specs,
        scratch_shapes=scratch,
        cost_estimate=pl.CostEstimate(flops=flops, bytes_accessed=size, transcendentals=0),
        compiler_params=pltpu.CompilerParams(vmem_limit_bytes=limit * 1024 * 1024),
    )(*operands)


def per_device(queries, keys, values, offsets):
    rows, width = queries.shape
    seq, sub = lax.axis_size("seq"), lax.axis_size("sub")
    sizes = Sizes(rows, seq, sub)

    def array(count, columns=width, dtype=jnp.bfloat16):
        return jax.ShapeDtypeStruct((count, columns), dtype)

    def swap(x, axis, mask):
        return lax.ppermute(x, axis, [(n, n ^ mask) for n in range(lax.axis_size(axis))])

    def after(x, *earlier):
        return lax.optimization_barrier((x, *earlier))[0]

    def far(x):
        return [swap(x, "sub", mask) for mask in range(2, sub, 2)]

    def both_cores(lines):
        chips = [[n, n + 1] for n in range(0, sub, 2)]
        return [lax.all_gather(x, "sub", axis=0, tiled=True, axis_index_groups=chips) for x in lines]

    masks = range(1, seq)
    heads = width // HEAD_DIMENSION
    q_kept, first, lanes = call(
        functools.partial(first_kernel, sizes),
        [array(sizes.kept_pad), array(sizes.first), array(round_up(heads, 8), 128, jnp.int32)],
        (offsets, queries, keys, values),
        COST[0],
        pltpu.HBM,
        [pltpu.SMEM(offsets.shape, jnp.int32)]
        + [pltpu.VMEM((rows, width), jnp.bfloat16)] * 3
        + [pltpu.SemaphoreType.DMA((4,))],
        LIMIT,
    )
    far_first = far(first)
    visitors = [swap(q_kept, "seq", mask) for mask in masks]
    q, own, second = call(
        functools.partial(order_kernel, sizes),
        [array(n) for n in (sizes.all_pad, 2 * sizes.all_pad, sizes.second)],
        (offsets, queries, keys, values),
        COST[5],
    )
    far_second = far(after(second, *far_first))
    own = [own, swap(own, "sub", 1)]
    far_first = both_cores(far_first)
    visitors = call(
        functools.partial(collect_kernel, len(masks)),
        array(len(masks) * sizes.kept_pad),
        (*visitors, *far_first),
        COST[4],
    )
    parts = call(
        functools.partial(partial_kernel, sizes, len(masks)),
        [array(sizes.kept_pad, width + PAIR)] * len(masks),
        (visitors, *own, *far_first),
        COST[1],
    )
    returned = [swap(part, "seq", mask) for mask, part in zip(masks, parts)]
    far_second = both_cores([after(x, parts[0]) for x in far_second])
    dense = call(
        functools.partial(dense_kernel, sizes),
        [
            array(sizes.all_pad, dtype=jnp.float32),
            array(sizes.all_pad, dtype=jnp.float32),
            array(sizes.kept_pad, dtype=jnp.float32),
            array(width // PAIR * 2 * rows, sizes.all_pad),
        ],
        (lanes, q, *own, *(x for both in zip(far_first, far_second) for x in both)),
        COST[2],
    )
    return call(functools.partial(merge_kernel, sizes), array(rows), (*dense, *returned), COST[3])


def solution(mesh):
    placed = P(("rep", "seq", "sub"), None)
    return jax.shard_map(
        per_device,
        mesh=mesh,
        in_specs=(placed, placed, placed, P()),
        out_specs=placed,
        check_vma=False,
    )
```

```python
import functools

import jax
import jax.numpy as jnp
from jax import lax
from jax.experimental import pallas as pl
from jax.experimental.pallas import tpu as pltpu
from jax.sharding import PartitionSpec as P

ATTENTION_HEADS = 12
HEAD_DIMENSION = 64
PAIR = 2 * HEAD_DIMENSION
LOWEST = -1e30
LIMIT = 56
COST = (10**6, 10**6, 10**10, 0, 0, 10**6, 10**6, 10**6)


def round_up(count, step):
    return -(-count // step) * step


class Sizes:
    def __init__(self, rows, dilation, sub):
        self.rows, self.dilation, self.sub = rows, dilation, sub
        self.kept = rows // dilation
        self.rest = rows - self.kept
        self.kept_pad = round_up(self.kept, 16)
        self.rest_pad = round_up(self.rest, 16)
        self.all_pad = self.kept_pad + self.rest_pad
        self.first = 2 * self.kept_pad
        self.second = 2 * self.rest_pad
        self.shift = dilation.bit_length() - 1
        self.kept_keys = sub * self.kept_pad
        self.keys = sub * self.all_pad
        self.padded = self.kept_pad != self.kept or self.rest_pad != self.rest


def target_rows(sizes, position, offset):
    residue = jnp.bitwise_and(position, sizes.dilation - 1)
    group = jnp.right_shift(position, sizes.shift)
    slab = jnp.bitwise_and(residue - offset + sizes.dilation, sizes.dilation - 1)
    return jnp.where(slab == 0, group, sizes.kept_pad + (slab - 1) * sizes.kept + group)


def order_rows(sizes, offset):
    shape = (sizes.all_pad, sizes.rows)
    place = lax.broadcasted_iota(jnp.int32, shape, 0)
    target = target_rows(sizes, lax.broadcasted_iota(jnp.int32, (1, sizes.rows), 1), offset)
    return jnp.where(place == target, 1.0, 0.0).astype(jnp.bfloat16)


def restore_rows(sizes, offset):
    shape = (sizes.rows, sizes.all_pad)
    place = lax.broadcasted_iota(jnp.int32, shape, 1)
    target = target_rows(sizes, lax.broadcasted_iota(jnp.int32, shape, 0), offset)
    return jnp.where(place == target, 1.0, 0.0).astype(jnp.bfloat16)


def first_head(shape):
    return lax.broadcasted_iota(jnp.int32, shape, 1) < HEAD_DIMENSION


def dot(a, b):
    return jnp.dot(a, b, preferred_element_type=jnp.float32)


def dot_rows(a, b):
    return lax.dot_general(a, b, (((1,), (1,)), ((), ())), preferred_element_type=jnp.float32)


def select(both, rows, columns=slice(0, PAIR)):
    return jnp.where(first_head((rows, PAIR)), both[:rows, columns], both[rows:, columns])


def order_rows_of_pair(sizes, offset, pair, count):
    return jnp.concatenate([order_rows(sizes, offset(2 * pair + n))[:count] for n in range(2)], 0)


def fetch(sources, targets, sems):
    copies = [pltpu.make_async_copy(s, t, sems.at[n]) for n, (s, t) in enumerate(zip(sources, targets))]
    for copy in copies:
        copy.start()
    for copy in copies:
        copy.wait()


def first_kernel(sizes, *refs):
    qd_ref, first_ref, second_ref, lanes_ref = refs[4:8]
    off_ref, q_ref, k_ref, v_ref, sems = refs[8:]
    fetch(refs[:4], (off_ref, q_ref, k_ref, v_ref), sems)
    kept, rest, count = sizes.kept_pad, sizes.rest_pad, sizes.all_pad
    scale = HEAD_DIMENSION ** (-0.5)
    lanes = lax.broadcasted_iota(jnp.int32, lanes_ref.shape, 0)
    spread_out = jnp.zeros(lanes_ref.shape, jnp.int32)
    for head in range(q_ref.shape[1] // HEAD_DIMENSION):
        spread_out = jnp.where(lanes == head, off_ref[head], spread_out)
    lanes_ref[...] = spread_out
    for pair in range(q_ref.shape[1] // PAIR):
        cols = slice(pair * PAIR, (pair + 1) * PAIR)
        chosen = order_rows_of_pair(sizes, lambda head: off_ref[head], pair, count)
        both = dot(chosen, jnp.concatenate([q_ref[:, cols], k_ref[:, cols], v_ref[:, cols]], 1))
        q = select(both, count)[:kept] * scale
        k = select(both, count, slice(PAIR, 2 * PAIR)).astype(jnp.bfloat16)
        v = select(both, count, slice(2 * PAIR, 3 * PAIR)).astype(jnp.bfloat16)
        qd_ref[:, cols] = q.astype(jnp.bfloat16)
        first_ref[:kept, cols] = k[:kept]
        first_ref[kept:, cols] = v[:kept]
        second_ref[:rest, cols] = k[kept:]
        second_ref[rest:, cols] = v[kept:]


def order_kernel(sizes, off_ref, q_ref, k_ref, v_ref, qs_ref, own_ref):
    kept, count = sizes.kept_pad, sizes.all_pad
    scale = HEAD_DIMENSION ** (-0.5)
    for pair in range(q_ref.shape[1] // PAIR):
        cols = slice(pair * PAIR, (pair + 1) * PAIR)
        chosen = order_rows_of_pair(sizes, lambda head: off_ref[head], pair, count)
        both = dot(chosen, jnp.concatenate([q_ref[:, cols], k_ref[:, cols], v_ref[:, cols]], 1))
        qs_ref[:, cols] = (select(both, count) * scale).astype(jnp.bfloat16)
        k = select(both, count, slice(PAIR, 2 * PAIR)).astype(jnp.bfloat16)
        v = select(both, count, slice(2 * PAIR, 3 * PAIR)).astype(jnp.bfloat16)
        own_ref[:, cols] = jnp.concatenate([k[:kept], v[:kept], k[kept:], v[kept:]], 0)


def rows_of(device, begin, count, cols):
    found = []
    for ref, base, size in device:
        low, high = max(begin, 0), min(begin + count, size)
        if low < high:
            found.append(ref[base + low : base + high, cols])
        begin -= size
    return found


def both_heads(q):
    mask = first_head(q.shape)
    zero = jnp.zeros_like(q)
    return jnp.concatenate([jnp.where(mask, q, zero), jnp.where(mask, zero, q)], 0)


def with_ones(v):
    return jnp.concatenate([v, jnp.ones_like(v)], 1)


def hide(col, step, used):
    return jnp.where(lax.rem(col + step, step) < used, 0.0, LOWEST)


def weigh(scores, top, v):
    weights = jnp.exp(scores - top).astype(jnp.bfloat16)
    return dot(weights, with_ones(v))


def whole(ref):
    return [(ref, 0, ref.shape[0])]


def in_turn(sizes, ref):
    far = (sizes.sub - 2) // 2
    half = ref.shape[0] // 2
    lots = [[(ref, core * half + n * sizes.first, sizes.first)] for n in range(2 * far + 1) for core in range(2)]
    return lots[: 2 * far], lots[2 * far :]


def join(devices, begin, count, cols):
    return [x for d in devices for x in rows_of(d, begin, count, cols)]


def collect_kernel(count, *refs):
    inputs, outputs = refs[:-2], refs[-2:]
    for found, out in zip((inputs[:count], inputs[count:]), outputs):
        begin = 0
        for r in found:
            out[begin : begin + r.shape[0]] = r[...]
            begin += r.shape[0]


def partial_kernel(sizes, others, q_ref, visitor_ref, own_ref, core_ref, first_ref, *out_refs):
    here, beside = in_turn(sizes, first_ref)
    devices = [whole(own_ref), whole(core_ref)] + here + beside
    width = q_ref.shape[1]
    kept = sizes.kept_pad
    rows = (others + 1) * kept
    col = lax.broadcasted_iota(jnp.int32, (2 * rows, 2 * sizes.kept_keys), 1)
    row = lax.broadcasted_iota(jnp.int32, (2 * rows, 2 * sizes.kept_keys), 0)
    row = jnp.where(row < rows, row, row - rows)
    known = jnp.where(row >= others * kept, 1, 0) * jnp.where(col < sizes.kept_keys, 1, 0)
    hidden = jnp.where(known == 1, LOWEST, 0.0)
    if sizes.padded:
        hidden += hide(col, kept, sizes.kept)
    lane = lax.broadcasted_iota(jnp.int32, (rows, PAIR), 1)
    stats = jnp.zeros((rows, PAIR), jnp.float32)
    for pair in range(width // PAIR):
        cols = slice(pair * PAIR, (pair + 1) * PAIR)
        q = jnp.concatenate([visitor_ref[:, cols], q_ref[:kept, cols]], 0)
        k = jnp.concatenate(join(devices, 0, kept, cols), 0)
        v = jnp.concatenate(join(devices, kept, kept, cols), 0)
        scores = dot_rows(both_heads(q), k) + hidden
        top = jnp.max(scores, 1, keepdims=True).astype(jnp.bfloat16).astype(jnp.float32)
        both = weigh(scores, top, v)
        lead, follow = both[:rows], both[rows:]
        out = select(both, rows).astype(jnp.bfloat16)
        for n, r in enumerate(out_refs):
            r[:, cols] = out[n * kept : (n + 1) * kept]
        for n, part in enumerate((lead, follow)):
            head = 3 * (2 * pair + n)
            total = part[:, PAIR:]
            coarse = total.astype(jnp.bfloat16).astype(jnp.float32)
            stats = jnp.where(lane == head, top[n * rows : (n + 1) * rows], stats)
            stats = jnp.where(lane == head + 1, coarse, stats)
            stats = jnp.where(lane == head + 2, total - coarse, stats)
    stats = stats.astype(jnp.bfloat16)
    for n, r in enumerate(out_refs):
        r[:, width:] = stats[n * kept : (n + 1) * kept]


def dense_kernel(sizes, *refs):
    off_ref, q_ref = refs[:2]
    own_refs, first_ref, second_refs = refs[2:4], refs[4], refs[5:-4]
    devices = [whole(r) for r in own_refs]
    for n, d in enumerate(in_turn(sizes, first_ref)[0]):
        r = second_refs[n // 2]
        devices.append(d + [(r, n % 2 * sizes.second, sizes.second)])
    out_ref, total_ref, top_ref, back_ref = refs[-4:]
    width = q_ref.shape[1]
    kept, rest, rows = sizes.kept_pad, sizes.rest_pad, sizes.all_pad
    begin = sizes.kept_keys
    for pair in range(width // PAIR):
        cols = slice(pair * PAIR, (pair + 1) * PAIR)
        k = jnp.concatenate(join(devices, 0, kept, cols) + join(devices, 2 * kept, rest, cols), 0)
        v = jnp.concatenate(join(devices, kept, kept, cols) + join(devices, kept + rows, rest, cols), 0)
        scores = dot_rows(both_heads(q_ref[:, cols]), k)
        if sizes.padded:
            col = lax.broadcasted_iota(jnp.int32, (1, sizes.keys), 1)
            here = hide(col, kept, sizes.kept)
            there = hide(col - begin + sizes.keys * rest, rest, sizes.rest)
            scores += jnp.where(col < begin, here, there)
        top = jnp.max(scores, 1, keepdims=True)
        weights = jnp.exp(scores - top)
        near, far = weights[:, :begin], weights[:, begin:]
        near = jnp.concatenate(
            [near[:kept] * 2.0, near[kept:rows], near[rows : rows + kept] * 2.0, near[rows + kept :]], 0
        )
        weights = jnp.concatenate([near, far], 1).astype(jnp.bfloat16)
        both = dot(weights, with_ones(v))
        out_ref[:, cols] = select(both, rows)
        total_ref[:, cols] = select(both, rows, slice(PAIR, 2 * PAIR))
        top_ref[:, cols] = jnp.where(first_head((kept, PAIR)), top[:kept], top[rows : rows + kept])
        for n in range(2):
            place = 2 * pair + n
            back_ref[place * sizes.rows : (place + 1) * sizes.rows] = restore_rows(sizes, off_ref[place : place + 1, 0:1])


def spread(width, lanes):
    lane = lax.broadcasted_iota(jnp.int32, (PAIR, width), 0)
    head = jnp.right_shift(lax.broadcasted_iota(jnp.int32, (PAIR, width), 1), HEAD_DIMENSION.bit_length() - 1)
    hits = [jnp.where(lane == 3 * head + n, 1.0, 0.0) for n in lanes]
    return sum(hits).astype(jnp.bfloat16)


def merge_kernel(sizes, *refs):
    out_ref, total_ref, top_ref, back_ref = refs[:4]
    part_refs, done_ref = refs[4:-1], refs[-1]
    others = len(part_refs)
    width = out_ref.shape[1]
    kept = sizes.kept_pad
    stats = jnp.concatenate([r[:, width:] for r in part_refs], 0)
    tops = dot(stats, spread(width, (0,)))
    totals = dot(stats, spread(width, (1, 2)))
    results = []
    for pair in range(width // PAIR):
        cols = slice(pair * PAIR, (pair + 1) * PAIR)
        out, total = out_ref[:, cols], total_ref[:, cols]
        top = top_ref[:, cols]
        theirs = [tops[n * kept : (n + 1) * kept, cols] for n in range(others)]
        best = functools.reduce(jnp.maximum, theirs, top)
        factor = jnp.exp(top - best)
        kept_out, kept_total = out[:kept] * factor, total[:kept] * factor
        for n, r in enumerate(part_refs):
            factor = jnp.exp(theirs[n] - best)
            kept_out += r[:, cols].astype(jnp.float32) * factor
            kept_total += totals[n * kept : (n + 1) * kept, cols] * factor
        result = jnp.concatenate([kept_out / kept_total, out[kept:] / total[kept:]], 0)
        results.append(result.astype(jnp.bfloat16))
    for pair, result in enumerate(results):
        cols = slice(pair * PAIR, (pair + 1) * PAIR)
        back = dot(back_ref[2 * sizes.rows * pair : 2 * sizes.rows * (pair + 1)], result)
        done_ref[:, cols] = select(back, sizes.rows).astype(jnp.bfloat16)


def call(kernel, out_shape, operands, flops, place=pltpu.VMEM, scratch=(), limit=24):
    spec = pl.BlockSpec(memory_space=place)
    smem = pl.BlockSpec(memory_space=pltpu.SMEM)
    in_specs = [smem if x.ndim == 1 and place == pltpu.VMEM else spec for x in operands]
    out_specs = jax.tree.map(lambda _: pl.BlockSpec(memory_space=pltpu.VMEM), out_shape)
    size = sum(x.size * 2 for x in operands)
    return pl.pallas_call(
        kernel,
        out_shape=out_shape,
        in_specs=in_specs,
        out_specs=out_specs,
        scratch_shapes=scratch,
        cost_estimate=pl.CostEstimate(flops=flops, bytes_accessed=size, transcendentals=0),
        compiler_params=pltpu.CompilerParams(vmem_limit_bytes=limit * 1024 * 1024),
    )(*operands)


def per_device(queries, keys, values, offsets):
    rows, width = queries.shape
    seq, sub = lax.axis_size("seq"), lax.axis_size("sub")
    sizes = Sizes(rows, seq, sub)

    def array(count, columns=width, dtype=jnp.bfloat16):
        return jax.ShapeDtypeStruct((count, columns), dtype)

    def swap(x, axis, mask):
        return lax.ppermute(x, axis, [(n, n ^ mask) for n in range(lax.axis_size(axis))])

    def after(x, *earlier):
        return lax.optimization_barrier((x, *earlier))[0]

    def far(x):
        return [swap(x, "sub", mask) for mask in range(2, sub, 2)]

    def both_cores(lines):
        chips = [[n, n + 1] for n in range(0, sub, 2)]
        return [lax.all_gather(x, "sub", axis=0, tiled=True, axis_index_groups=chips) for x in lines]

    def swap_both(x, mask):
        size = seq * sub
        return lax.ppermute(x, ("seq", "sub"), [(n, n ^ sub ^ mask) for n in range(size)])

    masks, far_masks = range(2, seq, 2), range(2, sub, 2)
    heads = width // HEAD_DIMENSION
    q_kept, first, second, lanes = call(
        functools.partial(first_kernel, sizes),
        [array(n) for n in (sizes.kept_pad, sizes.first, sizes.second)]
        + [array(round_up(heads, 8), 128, jnp.int32)],
        (offsets, queries, keys, values),
        COST[0],
        pltpu.HBM,
        [pltpu.SMEM(offsets.shape, jnp.int32)]
        + [pltpu.VMEM((rows, width), jnp.bfloat16)] * 3
        + [pltpu.SemaphoreType.DMA((4,))],
        LIMIT,
    )
    lot = far(first) + [swap(first, "seq", 1)] + [swap_both(first, mask) for mask in far_masks]
    visitors = [swap(q_kept, "seq", mask) for mask in masks]
    far_second = far(second)
    q, own = call(
        functools.partial(order_kernel, sizes),
        [array(n) for n in (sizes.all_pad, 2 * sizes.all_pad)],
        (offsets, queries, keys, values),
        COST[1],
    )
    own = [own, swap(own, "sub", 1)]
    lot, visitors = call(
        functools.partial(collect_kernel, len(lot)),
        [array(len(lot) * sizes.first), array(len(masks) * sizes.kept_pad)],
        (*lot, *visitors),
        COST[2],
    )
    (lot,) = both_cores([lot])
    *parts, own_part = call(
        functools.partial(partial_kernel, sizes, len(masks)),
        [array(sizes.kept_pad, width + PAIR)] * (len(masks) + 1),
        (q, visitors, *own, lot),
        COST[5],
    )
    returned = [swap(part, "seq", mask) for mask, part in zip(masks, parts)]
    far_second = both_cores([after(x, *parts) for x in far_second])
    dense = call(
        functools.partial(dense_kernel, sizes),
        [
            array(sizes.all_pad, dtype=jnp.float32),
            array(sizes.all_pad, dtype=jnp.float32),
            array(sizes.kept_pad, dtype=jnp.float32),
            array(width // PAIR * 2 * rows, sizes.all_pad),
        ],
        (lanes, q, *own, lot, *far_second),
        COST[6],
    )
    return call(functools.partial(merge_kernel, sizes), array(rows), (*dense, *returned, own_part), COST[7])


def solution(mesh):
    placed = P(("rep", "seq", "sub"), None)
    return jax.shard_map(
        per_device,
        mesh=mesh,
        in_specs=(placed, placed, placed, P()),
        out_specs=placed,
        check_vma=False,
    )
```

```python
import functools

import jax
import jax.numpy as jnp
from jax import lax
from jax.experimental import pallas as pl
from jax.experimental.pallas import tpu as pltpu
from jax.sharding import PartitionSpec as P

ATTENTION_HEADS = 12
HEAD_DIMENSION = 64
PAIR = 2 * HEAD_DIMENSION
LOWEST = -1e30
LIMIT = 56
COST = (10**6, 10**6, 10**10, 0, 0, 10**6, 10**6, 10**6)


def round_up(count, step):
    return -(-count // step) * step


class Sizes:
    def __init__(self, rows, dilation, sub):
        self.rows, self.dilation, self.sub = rows, dilation, sub
        self.kept = rows // dilation
        self.rest = rows - self.kept
        self.kept_pad = round_up(self.kept, 16)
        self.rest_pad = round_up(self.rest, 16)
        self.all_pad = self.kept_pad + self.rest_pad
        self.first = 2 * self.kept_pad
        self.second = 2 * self.rest_pad
        self.shift = dilation.bit_length() - 1
        self.kept_keys = sub * self.kept_pad
        self.keys = sub * self.all_pad
        self.padded = self.kept_pad != self.kept or self.rest_pad != self.rest


def target_rows(sizes, position, offset):
    residue = jnp.bitwise_and(position, sizes.dilation - 1)
    group = jnp.right_shift(position, sizes.shift)
    slab = jnp.bitwise_and(residue - offset + sizes.dilation, sizes.dilation - 1)
    return jnp.where(slab == 0, group, sizes.kept_pad + (slab - 1) * sizes.kept + group)


def order_rows(sizes, offset):
    shape = (sizes.all_pad, sizes.rows)
    place = lax.broadcasted_iota(jnp.int32, shape, 0)
    target = target_rows(sizes, lax.broadcasted_iota(jnp.int32, (1, sizes.rows), 1), offset)
    return jnp.where(place == target, 1.0, 0.0).astype(jnp.bfloat16)


def restore_rows(sizes, offset):
    shape = (sizes.rows, sizes.all_pad)
    place = lax.broadcasted_iota(jnp.int32, shape, 1)
    target = target_rows(sizes, lax.broadcasted_iota(jnp.int32, shape, 0), offset)
    return jnp.where(place == target, 1.0, 0.0).astype(jnp.bfloat16)


def first_head(shape):
    return lax.broadcasted_iota(jnp.int32, shape, 1) < HEAD_DIMENSION


def dot(a, b):
    return jnp.dot(a, b, preferred_element_type=jnp.float32)


def dot_rows(a, b):
    return lax.dot_general(a, b, (((1,), (1,)), ((), ())), preferred_element_type=jnp.float32)


def select(both, rows, columns=slice(0, PAIR)):
    return jnp.where(first_head((rows, PAIR)), both[:rows, columns], both[rows:, columns])


def order_rows_of_pair(sizes, offset, pair, count):
    return jnp.concatenate([order_rows(sizes, offset(2 * pair + n))[:count] for n in range(2)], 0)


def fetch(sources, targets, sems):
    copies = [pltpu.make_async_copy(s, t, sems.at[n]) for n, (s, t) in enumerate(zip(sources, targets))]
    for copy in copies:
        copy.start()
    for copy in copies:
        copy.wait()


def first_kernel(sizes, *refs):
    qd_ref, first_ref, second_ref, lanes_ref = refs[4:8]
    off_ref, q_ref, k_ref, v_ref, sems = refs[8:]
    fetch(refs[:4], (off_ref, q_ref, k_ref, v_ref), sems)
    kept, rest, count = sizes.kept_pad, sizes.rest_pad, sizes.all_pad
    scale = HEAD_DIMENSION ** (-0.5)
    lanes = lax.broadcasted_iota(jnp.int32, lanes_ref.shape, 0)
    spread_out = jnp.zeros(lanes_ref.shape, jnp.int32)
    for head in range(q_ref.shape[1] // HEAD_DIMENSION):
        spread_out = jnp.where(lanes == head, off_ref[head], spread_out)
    lanes_ref[...] = spread_out
    for pair in range(q_ref.shape[1] // PAIR):
        cols = slice(pair * PAIR, (pair + 1) * PAIR)
        chosen = order_rows_of_pair(sizes, lambda head: off_ref[head], pair, count)
        both = dot(chosen, jnp.concatenate([q_ref[:, cols], k_ref[:, cols], v_ref[:, cols]], 1))
        q = select(both, count)[:kept] * scale
        k = select(both, count, slice(PAIR, 2 * PAIR)).astype(jnp.bfloat16)
        v = select(both, count, slice(2 * PAIR, 3 * PAIR)).astype(jnp.bfloat16)
        qd_ref[:, cols] = q.astype(jnp.bfloat16)
        first_ref[:kept, cols] = k[:kept]
        first_ref[kept:, cols] = v[:kept]
        second_ref[:rest, cols] = k[kept:]
        second_ref[rest:, cols] = v[kept:]


def order_kernel(sizes, off_ref, q_ref, k_ref, v_ref, qs_ref, own_ref):
    kept, count = sizes.kept_pad, sizes.all_pad
    scale = HEAD_DIMENSION ** (-0.5)
    found = []
    for pair in range(q_ref.shape[1] // PAIR):
        cols = slice(pair * PAIR, (pair + 1) * PAIR)
        chosen = order_rows_of_pair(sizes, lambda head: off_ref[head], pair, count)
        found.append(dot(chosen, jnp.concatenate([q_ref[:, cols], k_ref[:, cols], v_ref[:, cols]], 1)))
    for pair, both in enumerate(found):
        cols = slice(pair * PAIR, (pair + 1) * PAIR)
        qs_ref[:, cols] = (select(both, count) * scale).astype(jnp.bfloat16)
        k = select(both, count, slice(PAIR, 2 * PAIR)).astype(jnp.bfloat16)
        v = select(both, count, slice(2 * PAIR, 3 * PAIR)).astype(jnp.bfloat16)
        own_ref[:, cols] = jnp.concatenate([k[:kept], v[:kept], k[kept:], v[kept:]], 0)


def rows_of(device, begin, count, cols):
    found = []
    for ref, base, size in device:
        low, high = max(begin, 0), min(begin + count, size)
        if low < high:
            found.append(ref[base + low : base + high, cols])
        begin -= size
    return found


def both_heads(q):
    mask = first_head(q.shape)
    zero = jnp.zeros_like(q)
    return jnp.concatenate([jnp.where(mask, q, zero), jnp.where(mask, zero, q)], 0)


def with_ones(v):
    return jnp.concatenate([v, jnp.ones_like(v)], 1)


def hide(col, step, used):
    return jnp.where(lax.rem(col + step, step) < used, 0.0, LOWEST)


def weigh(scores, top, v):
    weights = jnp.exp(scores - top).astype(jnp.bfloat16)
    return dot(weights, with_ones(v))


def whole(ref):
    return [(ref, 0, ref.shape[0])]


def in_turn(sizes, refs):
    found = [[(r, 0, sizes.first)] for r in refs]
    return found[: sizes.sub - 2], found[sizes.sub - 2 :]


def join(devices, begin, count, cols):
    return [x for d in devices for x in rows_of(d, begin, count, cols)]


def collect_kernel(count, *refs):
    begin = 0
    for r in refs[:count]:
        refs[-1][begin : begin + r.shape[0]] = r[...]
        begin += r.shape[0]


def partial_kernel(sizes, others, q_ref, visitor_ref, own_ref, core_ref, *refs):
    first_refs, out_refs = refs[: -others - 1], refs[-others - 1 :]
    here, beside = in_turn(sizes, first_refs)
    devices = [whole(own_ref), whole(core_ref)] + here + beside
    width = q_ref.shape[1]
    kept = sizes.kept_pad
    rows = (others + 1) * kept
    col = lax.broadcasted_iota(jnp.int32, (2 * rows, 2 * sizes.kept_keys), 1)
    row = lax.broadcasted_iota(jnp.int32, (2 * rows, 2 * sizes.kept_keys), 0)
    row = jnp.where(row < rows, row, row - rows)
    known = jnp.where(row >= others * kept, 1, 0) * jnp.where(col < sizes.kept_keys, 1, 0)
    hidden = jnp.where(known == 1, LOWEST, 0.0)
    if sizes.padded:
        hidden += hide(col, kept, sizes.kept)
    lane = lax.broadcasted_iota(jnp.int32, (rows, PAIR), 1)
    stats = jnp.zeros((rows, PAIR), jnp.float32)
    for pair in range(width // PAIR):
        cols = slice(pair * PAIR, (pair + 1) * PAIR)
        q = jnp.concatenate([visitor_ref[:, cols], q_ref[:kept, cols]], 0)
        k = jnp.concatenate(join(devices, 0, kept, cols), 0)
        v = jnp.concatenate(join(devices, kept, kept, cols), 0)
        scores = dot_rows(both_heads(q), k) + hidden
        top = jnp.max(scores, 1, keepdims=True).astype(jnp.bfloat16).astype(jnp.float32)
        both = weigh(scores, top, v)
        lead, follow = both[:rows], both[rows:]
        out = select(both, rows).astype(jnp.bfloat16)
        for n, r in enumerate(out_refs):
            r[:, cols] = out[n * kept : (n + 1) * kept]
        for n, part in enumerate((lead, follow)):
            head = 3 * (2 * pair + n)
            total = part[:, PAIR:]
            coarse = total.astype(jnp.bfloat16).astype(jnp.float32)
            stats = jnp.where(lane == head, top[n * rows : (n + 1) * rows], stats)
            stats = jnp.where(lane == head + 1, coarse, stats)
            stats = jnp.where(lane == head + 2, total - coarse, stats)
    stats = stats.astype(jnp.bfloat16)
    for n, r in enumerate(out_refs):
        r[:, width:] = stats[n * kept : (n + 1) * kept]


def dense_kernel(sizes, *refs):
    off_ref, q_ref = refs[:2]
    own_refs, first_refs, second_refs = refs[2:4], refs[4 : 2 + sizes.sub], refs[2 + sizes.sub : -5]
    devices = [whole(r) for r in own_refs]
    for n, d in enumerate(in_turn(sizes, first_refs)[0]):
        r = second_refs[n // 2]
        devices.append(d + [(r, n % 2 * sizes.second, sizes.second)])
    base_ref, out_ref, total_ref, top_ref, back_ref = refs[-5:]
    width = q_ref.shape[1]
    kept, rest, rows = sizes.kept_pad, sizes.rest_pad, sizes.all_pad
    begin = sizes.kept_keys
    results = []
    for pair in range(width // PAIR):
        cols = slice(pair * PAIR, (pair + 1) * PAIR)
        k = jnp.concatenate(join(devices, 0, kept, cols) + join(devices, 2 * kept, rest, cols), 0)
        v = jnp.concatenate(join(devices, kept, kept, cols) + join(devices, kept + rows, rest, cols), 0)
        scores = dot_rows(both_heads(q_ref[:, cols]), k)
        if sizes.padded:
            col = lax.broadcasted_iota(jnp.int32, (1, sizes.keys), 1)
            here = hide(col, kept, sizes.kept)
            there = hide(col - begin + sizes.keys * rest, rest, sizes.rest)
            scores += jnp.where(col < begin, here, there)
        top = jnp.max(scores, 1, keepdims=True)
        weights = jnp.exp(scores - top)
        near, far = weights[:, :begin], weights[:, begin:]
        near = jnp.concatenate(
            [near[:kept] * 2.0, near[kept:rows], near[rows : rows + kept] * 2.0, near[rows + kept :]], 0
        )
        weights = jnp.concatenate([near, far], 1).astype(jnp.bfloat16)
        both = dot(weights, with_ones(v))
        out, total = select(both, rows), select(both, rows, slice(PAIR, 2 * PAIR))
        out_ref[:, cols], total_ref[:, cols] = out[:kept], total[:kept]
        top_ref[:, cols] = jnp.where(first_head((kept, PAIR)), top[:kept], top[rows : rows + kept])
        results.append((out[kept:] / total[kept:]).astype(jnp.bfloat16))
    for pair, result in enumerate(results):
        cols = slice(pair * PAIR, (pair + 1) * PAIR)
        back = [restore_rows(sizes, off_ref[2 * pair + n : 2 * pair + n + 1, 0:1]) for n in range(2)]
        back = jnp.concatenate(back, 0)
        back_ref[2 * sizes.rows * pair : 2 * sizes.rows * (pair + 1)] = back[:, :kept]
        whole_rows = jnp.concatenate([jnp.zeros((kept, PAIR), jnp.bfloat16), result], 0)
        base_ref[:, cols] = select(dot(back, whole_rows), sizes.rows).astype(jnp.bfloat16)


def dense_shapes(sizes, width):
    shapes = [(sizes.rows, width, jnp.bfloat16)]
    shapes += [(sizes.kept_pad, width, jnp.float32)] * 3
    shapes += [(width // PAIR * 2 * sizes.rows, sizes.kept_pad, jnp.bfloat16)]
    return [jax.ShapeDtypeStruct(s[:2], s[2]) for s in shapes]


def spread(width, lanes):
    lane = lax.broadcasted_iota(jnp.int32, (PAIR, width), 0)
    head = jnp.right_shift(lax.broadcasted_iota(jnp.int32, (PAIR, width), 1), HEAD_DIMENSION.bit_length() - 1)
    hits = [jnp.where(lane == 3 * head + n, 1.0, 0.0) for n in lanes]
    return sum(hits).astype(jnp.bfloat16)


def merge_kernel(sizes, *refs):
    base_ref, out_ref, total_ref, top_ref, back_ref = refs[:5]
    part_refs, done_ref = refs[5:-1], refs[-1]
    others = len(part_refs)
    width = out_ref.shape[1]
    kept = sizes.kept_pad
    stats = jnp.concatenate([r[:, width:] for r in part_refs], 0)
    tops = dot(stats, spread(width, (0,)))
    totals = dot(stats, spread(width, (1, 2)))
    theirs = [tops[n * kept : (n + 1) * kept] for n in range(others)]
    top = top_ref[...]
    best = functools.reduce(jnp.maximum, theirs, top)
    factor = jnp.exp(top - best)
    out, total = out_ref[...] * factor, total_ref[...] * factor
    for n, r in enumerate(part_refs):
        factor = jnp.exp(theirs[n] - best)
        out += r[:, :width].astype(jnp.float32) * factor
        total += totals[n * kept : (n + 1) * kept] * factor
    result = (out / total).astype(jnp.bfloat16)
    for pair in range(width // PAIR):
        cols = slice(pair * PAIR, (pair + 1) * PAIR)
        back = dot(back_ref[2 * sizes.rows * pair : 2 * sizes.rows * (pair + 1)], result[:, cols])
        done_ref[:, cols] = (select(back, sizes.rows) + base_ref[:, cols].astype(jnp.float32)).astype(jnp.bfloat16)


def call(kernel, out_shape, operands, flops, place=pltpu.VMEM, scratch=(), limit=24):
    spec = pl.BlockSpec(memory_space=place)
    smem = pl.BlockSpec(memory_space=pltpu.SMEM)
    in_specs = [smem if x.ndim == 1 and place == pltpu.VMEM else spec for x in operands]
    out_specs = jax.tree.map(lambda _: pl.BlockSpec(memory_space=pltpu.VMEM), out_shape)
    size = sum(x.size * 2 for x in operands)
    return pl.pallas_call(
        kernel,
        out_shape=out_shape,
        in_specs=in_specs,
        out_specs=out_specs,
        scratch_shapes=scratch,
        cost_estimate=pl.CostEstimate(flops=flops, bytes_accessed=size, transcendentals=0),
        compiler_params=pltpu.CompilerParams(vmem_limit_bytes=int(limit * 1024 * 1024)),
    )(*operands)


def per_device(queries, keys, values, offsets):
    rows, width = queries.shape
    seq, sub = lax.axis_size("seq"), lax.axis_size("sub")
    sizes = Sizes(rows, seq, sub)

    def array(count, columns=width, dtype=jnp.bfloat16):
        return jax.ShapeDtypeStruct((count, columns), dtype)

    def swap(x, axis, mask):
        return lax.ppermute(x, axis, [(n, n ^ mask) for n in range(lax.axis_size(axis))])

    def after(x, *earlier):
        return lax.optimization_barrier((x, *earlier))[0]

    def far(x):
        return [swap(x, "sub", mask) for mask in range(2, sub, 2)]

    def both_cores(lines):
        chips = [[n, n + 1] for n in range(0, sub, 2)]
        return [lax.all_gather(x, "sub", axis=0, tiled=True, axis_index_groups=chips) for x in lines]

    def swap_both(x, mask):
        size = seq * sub
        return lax.ppermute(x, ("seq", "sub"), [(n, n ^ sub ^ mask) for n in range(size)])

    masks, far_masks = range(2, seq, 2), range(2, sub, 2)
    heads = width // HEAD_DIMENSION
    q_kept, first, second, lanes = call(
        functools.partial(first_kernel, sizes),
        [array(n) for n in (sizes.kept_pad, sizes.first, sizes.second)]
        + [array(round_up(heads, 8), 128, jnp.int32)],
        (offsets, queries, keys, values),
        COST[0],
        pltpu.HBM,
        [pltpu.SMEM(offsets.shape, jnp.int32)]
        + [pltpu.VMEM((rows, width), jnp.bfloat16)] * 3
        + [pltpu.SemaphoreType.DMA((4,))],
        LIMIT,
    )
    lot = far(first) + [swap(first, "seq", 1)] + [swap_both(first, mask) for mask in far_masks]
    visitors = [swap(q_kept, "seq", mask) for mask in masks]
    far_second = far(second)
    q, own = call(
        functools.partial(order_kernel, sizes),
        [array(n) for n in (sizes.all_pad, 2 * sizes.all_pad)],
        (offsets, queries, keys, values),
        COST[1],
    )
    own = [own, swap(own, "sub", 1)]
    visitors = call(
        functools.partial(collect_kernel, len(masks)),
        array(len(masks) * sizes.kept_pad),
        (*visitors, *lot),
        COST[2],
    )
    lot = [y for x in lot for y in (x, swap(after(x, visitors), "sub", 1))]
    *parts, own_part = call(
        functools.partial(partial_kernel, sizes, len(masks)),
        [array(sizes.kept_pad, width + PAIR)] * (len(masks) + 1),
        (q, visitors, *own, *lot),
        COST[5],
    )
    returned = [swap(part, "seq", mask) for mask, part in zip(masks, parts)]
    far_second = both_cores([after(x, *parts) for x in far_second])
    dense = call(
        functools.partial(dense_kernel, sizes),
        dense_shapes(sizes, width),
        (lanes, q, *own, *lot[: sub - 2], *far_second),
        COST[6],
    )
    return call(functools.partial(merge_kernel, sizes), array(rows), (*dense, *returned, own_part), COST[7])


def solution(mesh):
    placed = P(("rep", "seq", "sub"), None)
    return jax.shard_map(
        per_device,
        mesh=mesh,
        in_specs=(placed, placed, placed, P()),
        out_specs=placed,
        check_vma=False,
    )
```

```python
import functools

import jax
import jax.numpy as jnp
from jax import lax
from jax.experimental import pallas as pl
from jax.experimental.pallas import tpu as pltpu
from jax.sharding import PartitionSpec as P

ATTENTION_HEADS = 12
HEAD_DIMENSION = 64
PAIR = 2 * HEAD_DIMENSION
LOWEST = -1e30
LIMIT = 56
COST = (10**6, 10**6, 10**10, 10**10, 0, 10**6, 10**6, 10**6)


def round_up(count, step):
    return -(-count // step) * step


class Sizes:
    def __init__(self, rows, dilation, sub):
        self.rows, self.dilation, self.sub = rows, dilation, sub
        self.kept = rows // dilation
        self.rest = rows - self.kept
        self.kept_pad = round_up(self.kept, 16)
        self.rest_pad = round_up(self.rest, 16)
        self.all_pad = self.kept_pad + self.rest_pad
        self.first = 2 * self.kept_pad
        self.second = 2 * self.rest_pad
        self.shift = dilation.bit_length() - 1
        self.kept_keys = sub * self.kept_pad
        self.keys = sub * self.all_pad
        self.padded = self.kept_pad != self.kept or self.rest_pad != self.rest


def target_rows(sizes, position, offset):
    residue = jnp.bitwise_and(position, sizes.dilation - 1)
    group = jnp.right_shift(position, sizes.shift)
    slab = jnp.bitwise_and(residue - offset + sizes.dilation, sizes.dilation - 1)
    return jnp.where(slab == 0, group, sizes.kept_pad + (slab - 1) * sizes.kept + group)


def order_rows(sizes, offset):
    shape = (sizes.all_pad, sizes.rows)
    place = lax.broadcasted_iota(jnp.int32, shape, 0)
    target = target_rows(sizes, lax.broadcasted_iota(jnp.int32, (1, sizes.rows), 1), offset)
    return jnp.where(place == target, 1.0, 0.0).astype(jnp.bfloat16)


def restore_rows(sizes, offset):
    shape = (sizes.rows, sizes.all_pad)
    place = lax.broadcasted_iota(jnp.int32, shape, 1)
    target = target_rows(sizes, lax.broadcasted_iota(jnp.int32, shape, 0), offset)
    return jnp.where(place == target, 1.0, 0.0).astype(jnp.bfloat16)


def first_head(shape):
    return lax.broadcasted_iota(jnp.int32, shape, 1) < HEAD_DIMENSION


def dot(a, b):
    return jnp.dot(a, b, preferred_element_type=jnp.float32)


def dot_rows(a, b):
    return lax.dot_general(a, b, (((1,), (1,)), ((), ())), preferred_element_type=jnp.float32)


def select(both, rows, columns=slice(0, PAIR)):
    return jnp.where(first_head((rows, PAIR)), both[:rows, columns], both[rows:, columns])


def order_rows_of_pair(sizes, offset, pair, count):
    return jnp.concatenate([order_rows(sizes, offset(2 * pair + n))[:count] for n in range(2)], 0)


def fetch(sources, targets, sems):
    copies = [pltpu.make_async_copy(s, t, sems.at[n]) for n, (s, t) in enumerate(zip(sources, targets))]
    for copy in copies:
        copy.start()
    for copy in copies:
        copy.wait()


def first_kernel(sizes, *refs):
    qd_ref, first_ref, second_ref = refs[4:7]
    off_ref, q_ref, k_ref, v_ref, sems = refs[7:]
    fetch(refs[:4], (off_ref, q_ref, k_ref, v_ref), sems)
    kept, rest, count = sizes.kept_pad, sizes.rest_pad, sizes.all_pad
    scale = HEAD_DIMENSION ** (-0.5)
    for pair in range(q_ref.shape[1] // PAIR):
        cols = slice(pair * PAIR, (pair + 1) * PAIR)
        chosen = order_rows_of_pair(sizes, lambda head: off_ref[head], pair, count)
        both = dot(chosen, jnp.concatenate([q_ref[:, cols], k_ref[:, cols], v_ref[:, cols]], 1))
        q = select(both, count)[:kept] * scale
        k = select(both, count, slice(PAIR, 2 * PAIR)).astype(jnp.bfloat16)
        v = select(both, count, slice(2 * PAIR, 3 * PAIR)).astype(jnp.bfloat16)
        qd_ref[:, cols] = q.astype(jnp.bfloat16)
        first_ref[:kept, cols] = k[:kept]
        first_ref[kept:, cols] = v[:kept]
        second_ref[:rest, cols] = k[kept:]
        second_ref[rest:, cols] = v[kept:]


def order_kernel(sizes, off_ref, q_ref, qs_ref, back_ref, spread_ref):
    width = q_ref.shape[1]
    scale = HEAD_DIMENSION ** (-0.5)
    for pair in range(width // PAIR):
        cols = slice(pair * PAIR, (pair + 1) * PAIR)
        chosen = order_rows_of_pair(sizes, lambda head: off_ref[head], pair, sizes.all_pad)
        qs_ref[:, cols] = (select(dot(chosen, q_ref[:, cols]), sizes.all_pad) * scale).astype(jnp.bfloat16)
        for head in (2 * pair, 2 * pair + 1):
            back_ref[head * sizes.rows : (head + 1) * sizes.rows] = restore_rows(sizes, off_ref[head])
    spread_ref[:, :width] = spread(width, (0,))
    spread_ref[:, width:] = spread(width, (1, 2))


def rows_of(device, begin, count, cols):
    found = []
    for ref, base, size in device:
        low, high = max(begin, 0), min(begin + count, size)
        if low < high:
            found.append(ref[base + low : base + high, cols])
        begin -= size
    return found


def both_heads(q):
    mask = first_head(q.shape)
    zero = jnp.zeros_like(q)
    return jnp.concatenate([jnp.where(mask, q, zero), jnp.where(mask, zero, q)], 0)


def with_ones(v):
    return jnp.concatenate([v, jnp.ones_like(v)], 1)


def hide(col, step, used):
    return jnp.where(lax.rem(col + step, step) < used, 0.0, LOWEST)


def weigh(scores, top, v):
    weights = jnp.exp(scores - top).astype(jnp.bfloat16)
    return dot(weights, with_ones(v))


def whole(ref):
    return [(ref, 0, ref.shape[0])]


def in_turn(sizes, refs):
    found = [[(r, n * sizes.first, sizes.first)] for n in range(sizes.sub) for r in refs]
    return found[: sizes.sub], found[sizes.sub :]


def join(devices, begin, count, cols):
    return [x for d in devices for x in rows_of(d, begin, count, cols)]


def collect_kernel(count, *refs):
    begin = 0
    for r in refs[:count]:
        refs[-1][begin : begin + r.shape[0]] = r[...]
        begin += r.shape[0]


def partial_kernel(sizes, others, q_ref, visitor_ref, lot_ref, other_lot_ref, *out_refs):
    here, beside = in_turn(sizes, (lot_ref, other_lot_ref))
    devices = here + beside
    width = q_ref.shape[1]
    kept = sizes.kept_pad
    rows = (others + 1) * kept
    col = lax.broadcasted_iota(jnp.int32, (2 * rows, 2 * sizes.kept_keys), 1)
    row = lax.broadcasted_iota(jnp.int32, (2 * rows, 2 * sizes.kept_keys), 0)
    row = jnp.where(row < rows, row, row - rows)
    known = jnp.where(row >= others * kept, 1, 0) * jnp.where(col < sizes.kept_keys, 1, 0)
    hidden = jnp.where(known == 1, LOWEST, 0.0)
    if sizes.padded:
        hidden += hide(col, kept, sizes.kept)
    lane = lax.broadcasted_iota(jnp.int32, (rows, PAIR), 1)
    stats = jnp.zeros((rows, PAIR), jnp.float32)
    for pair in range(width // PAIR):
        cols = slice(pair * PAIR, (pair + 1) * PAIR)
        q = jnp.concatenate([visitor_ref[:, cols], q_ref[:kept, cols]], 0)
        k = jnp.concatenate(join(devices, 0, kept, cols), 0)
        v = jnp.concatenate(join(devices, kept, kept, cols), 0)
        scores = dot_rows(both_heads(q), k) + hidden
        top = jnp.max(scores, 1, keepdims=True).astype(jnp.bfloat16).astype(jnp.float32)
        both = weigh(scores, top, v)
        lead, follow = both[:rows], both[rows:]
        out = select(both, rows).astype(jnp.bfloat16)
        for n, r in enumerate(out_refs):
            r[:, cols] = out[n * kept : (n + 1) * kept]
        for n, part in enumerate((lead, follow)):
            head = 3 * (2 * pair + n)
            total = part[:, PAIR:]
            coarse = total.astype(jnp.bfloat16).astype(jnp.float32)
            stats = jnp.where(lane == head, top[n * rows : (n + 1) * rows], stats)
            stats = jnp.where(lane == head + 1, coarse, stats)
            stats = jnp.where(lane == head + 2, total - coarse, stats)
    stats = stats.astype(jnp.bfloat16)
    for n, r in enumerate(out_refs):
        r[:, width:] = stats[n * kept : (n + 1) * kept]


def dense_kernel(sizes, *refs):
    back_ref, q_ref = refs[:2]
    lot_refs, near_refs, far_refs = refs[2:4], refs[4:6], refs[6:-4]
    second = [whole(r) for r in near_refs]
    second += [[(r, core * sizes.second, sizes.second)] for r in far_refs for core in range(2)]
    devices = [d + more for d, more in zip(in_turn(sizes, lot_refs)[0], second)]
    base_ref, out_ref, total_ref, top_ref = refs[-4:]
    width = q_ref.shape[1]
    kept, rest, rows = sizes.kept_pad, sizes.rest_pad, sizes.all_pad
    begin = sizes.kept_keys
    results = []
    for pair in range(width // PAIR):
        cols = slice(pair * PAIR, (pair + 1) * PAIR)
        k = jnp.concatenate(join(devices, 0, kept, cols) + join(devices, 2 * kept, rest, cols), 0)
        v = jnp.concatenate(join(devices, kept, kept, cols) + join(devices, kept + rows, rest, cols), 0)
        scores = dot_rows(both_heads(q_ref[:, cols]), k)
        if sizes.padded:
            col = lax.broadcasted_iota(jnp.int32, (1, sizes.keys), 1)
            here = hide(col, kept, sizes.kept)
            there = hide(col - begin + sizes.keys * rest, rest, sizes.rest)
            scores += jnp.where(col < begin, here, there)
        top = jnp.max(scores, 1, keepdims=True)
        weights = jnp.exp(scores - top)
        near, far = weights[:, :begin], weights[:, begin:]
        near = jnp.concatenate(
            [near[:kept] * 2.0, near[kept:rows], near[rows : rows + kept] * 2.0, near[rows + kept :]], 0
        )
        weights = jnp.concatenate([near, far], 1).astype(jnp.bfloat16)
        both = dot(weights, with_ones(v))
        out, total = select(both, rows), select(both, rows, slice(PAIR, 2 * PAIR))
        out_ref[:, cols], total_ref[:, cols] = out[:kept], total[:kept]
        top_ref[:, cols] = jnp.where(first_head((kept, PAIR)), top[:kept], top[rows : rows + kept])
        results.append((out[kept:] / total[kept:]).astype(jnp.bfloat16))
    for pair, result in enumerate(results):
        cols = slice(pair * PAIR, (pair + 1) * PAIR)
        back = back_ref[2 * sizes.rows * pair : 2 * sizes.rows * (pair + 1)]
        whole_rows = jnp.concatenate([jnp.zeros((kept, PAIR), jnp.bfloat16), result], 0)
        base_ref[:, cols] = select(dot(back, whole_rows), sizes.rows).astype(jnp.bfloat16)


def dense_shapes(sizes, width):
    shapes = [(sizes.rows, width, jnp.bfloat16)]
    shapes += [(sizes.kept_pad, width, jnp.float32)] * 3
    return [jax.ShapeDtypeStruct(s[:2], s[2]) for s in shapes]


def spread(width, lanes):
    lane = lax.broadcasted_iota(jnp.int32, (PAIR, width), 0)
    head = jnp.right_shift(lax.broadcasted_iota(jnp.int32, (PAIR, width), 1), HEAD_DIMENSION.bit_length() - 1)
    hits = [jnp.where(lane == 3 * head + n, 1.0, 0.0) for n in lanes]
    return sum(hits).astype(jnp.bfloat16)


def merge_kernel(sizes, *refs):
    back_ref, spread_ref, base_ref, out_ref, total_ref, top_ref = refs[:6]
    part_refs, done_ref = refs[6:-1], refs[-1]
    others = len(part_refs)
    width = out_ref.shape[1]
    kept = sizes.kept_pad
    stats = jnp.concatenate([r[:, width:] for r in part_refs], 0)
    tops = dot(stats, spread_ref[:, :width])
    totals = dot(stats, spread_ref[:, width:])
    theirs = [tops[n * kept : (n + 1) * kept] for n in range(others)]
    top = top_ref[...]
    best = functools.reduce(jnp.maximum, theirs, top)
    factor = jnp.exp(top - best)
    out, total = out_ref[...] * factor, total_ref[...] * factor
    for n, r in enumerate(part_refs):
        factor = jnp.exp(theirs[n] - best)
        out += r[:, :width].astype(jnp.float32) * factor
        total += totals[n * kept : (n + 1) * kept] * factor
    result = (out / total).astype(jnp.bfloat16)
    for pair in range(width // PAIR):
        cols = slice(pair * PAIR, (pair + 1) * PAIR)
        back = dot(back_ref[2 * sizes.rows * pair : 2 * sizes.rows * (pair + 1), :kept], result[:, cols])
        done_ref[:, cols] = (select(back, sizes.rows) + base_ref[:, cols].astype(jnp.float32)).astype(jnp.bfloat16)


def call(kernel, out_shape, operands, flops, place=pltpu.VMEM, scratch=(), limit=24):
    spec = pl.BlockSpec(memory_space=place)
    smem = pl.BlockSpec(memory_space=pltpu.SMEM)
    in_specs = [smem if x.ndim == 1 and place == pltpu.VMEM else spec for x in operands]
    out_specs = jax.tree.map(lambda _: pl.BlockSpec(memory_space=pltpu.VMEM), out_shape)
    size = sum(x.size * 2 for x in operands)
    return pl.pallas_call(
        kernel,
        out_shape=out_shape,
        in_specs=in_specs,
        out_specs=out_specs,
        scratch_shapes=scratch,
        cost_estimate=pl.CostEstimate(flops=flops, bytes_accessed=size, transcendentals=0),
        compiler_params=pltpu.CompilerParams(vmem_limit_bytes=int(limit * 1024 * 1024)),
    )(*operands)


def per_device(queries, keys, values, offsets):
    rows, width = queries.shape
    seq, sub = lax.axis_size("seq"), lax.axis_size("sub")
    sizes = Sizes(rows, seq, sub)

    def array(count, columns=width, dtype=jnp.bfloat16):
        return jax.ShapeDtypeStruct((count, columns), dtype)

    def swap(x, axis, mask):
        return lax.ppermute(x, axis, [(n, n ^ mask) for n in range(lax.axis_size(axis))])

    def after(x, *earlier):
        return lax.optimization_barrier((x, *earlier))[0]

    def far(x):
        return [swap(x, "sub", mask) for mask in range(2, sub, 2)]

    def both_cores(lines):
        chips = [[n, n + 1] for n in range(0, sub, 2)]
        return [lax.all_gather(x, "sub", axis=0, tiled=True, axis_index_groups=chips) for x in lines]

    def swap_both(x, mask):
        size = seq * sub
        return lax.ppermute(x, ("seq", "sub"), [(n, n ^ sub ^ mask) for n in range(size)])

    masks, far_masks = range(2, seq, 2), range(2, sub, 2)
    heads = width // HEAD_DIMENSION
    q_kept, first, second = call(
        functools.partial(first_kernel, sizes),
        [array(n) for n in (sizes.kept_pad, sizes.first, sizes.second)],
        (offsets, queries, keys, values),
        COST[0],
        pltpu.HBM,
        [pltpu.SMEM(offsets.shape, jnp.int32)]
        + [pltpu.VMEM((rows, width), jnp.bfloat16)] * 3
        + [pltpu.SemaphoreType.DMA((4,))],
        LIMIT,
    )
    far_first = far(first)
    lot = [first] + far_first + [swap(first, "seq", 1)] + [swap_both(first, mask) for mask in far_masks]
    far_second = far(second)
    q, back, spreads = call(
        functools.partial(order_kernel, sizes),
        [array(sizes.all_pad), array(heads * rows, sizes.all_pad), array(PAIR, 2 * width)],
        (offsets, queries),
        COST[1],
    )
    visitors = [swap(q_kept, "seq", mask) for mask in masks]
    lot = call(
        functools.partial(collect_kernel, len(lot)), array(len(lot) * sizes.first), (*lot, q), COST[2]
    )
    near_second = [second, swap(after(second, lot), "sub", 1)]
    lot = [lot, swap(lot, "sub", 1)]
    visitors = call(
        functools.partial(collect_kernel, len(masks)),
        array(len(masks) * sizes.kept_pad),
        visitors,
        COST[3],
    )
    *parts, own_part = call(
        functools.partial(partial_kernel, sizes, len(masks)),
        [array(sizes.kept_pad, width + PAIR)] * (len(masks) + 1),
        (q, visitors, *lot),
        COST[5],
    )
    returned = [swap(part, "seq", mask) for mask, part in zip(masks, parts)]
    far_second = both_cores([after(x, *parts) for x in far_second])
    dense = call(
        functools.partial(dense_kernel, sizes),
        dense_shapes(sizes, width),
        (back, q, *lot, *near_second, *far_second),
        COST[6],
    )
    return call(functools.partial(merge_kernel, sizes), array(rows), (back, spreads, *dense, *returned, own_part), COST[7])


def solution(mesh):
    placed = P(("rep", "seq", "sub"), None)
    return jax.shard_map(
        per_device,
        mesh=mesh,
        in_specs=(placed, placed, placed, P()),
        out_specs=placed,
        check_vma=False,
    )
```

```python
import functools

import jax
import jax.numpy as jnp
from jax import lax
from jax.experimental import pallas as pl
from jax.experimental.pallas import tpu as pltpu
from jax.sharding import PartitionSpec as P

ATTENTION_HEADS = 12
HEAD_DIMENSION = 64
PAIR = 2 * HEAD_DIMENSION
LOWEST = -1e30
LIMIT = 56
COST = (10**6, 10**6, 10**10, 10**10, 0, 10**6, 10**6, 10**6)


def round_up(count, step):
    return -(-count // step) * step


class Sizes:
    def __init__(self, rows, dilation, sub):
        self.rows, self.dilation, self.sub = rows, dilation, sub
        self.kept = rows // dilation
        self.rest = rows - self.kept
        self.kept_pad = round_up(self.kept, 16)
        self.rest_pad = round_up(self.rest, 16)
        self.all_pad = self.kept_pad + self.rest_pad
        self.first = 2 * self.kept_pad
        self.second = 2 * self.rest_pad
        self.shift = dilation.bit_length() - 1
        self.kept_keys = sub * self.kept_pad
        self.keys = sub * self.all_pad
        self.padded = self.kept_pad != self.kept or self.rest_pad != self.rest


def target_rows(sizes, position, offset):
    residue = jnp.bitwise_and(position, sizes.dilation - 1)
    group = jnp.right_shift(position, sizes.shift)
    slab = jnp.bitwise_and(residue - offset + sizes.dilation, sizes.dilation - 1)
    return jnp.where(slab == 0, group, sizes.kept_pad + (slab - 1) * sizes.kept + group)


def order_rows(sizes, offset):
    shape = (sizes.all_pad, sizes.rows)
    place = lax.broadcasted_iota(jnp.int32, shape, 0)
    target = target_rows(sizes, lax.broadcasted_iota(jnp.int32, (1, sizes.rows), 1), offset)
    return jnp.where(place == target, 1.0, 0.0).astype(jnp.bfloat16)


def restore_rows(sizes, offset):
    shape = (sizes.rows, sizes.all_pad)
    place = lax.broadcasted_iota(jnp.int32, shape, 1)
    target = target_rows(sizes, lax.broadcasted_iota(jnp.int32, shape, 0), offset)
    return jnp.where(place == target, 1.0, 0.0).astype(jnp.bfloat16)


def first_head(shape):
    return lax.broadcasted_iota(jnp.int32, shape, 1) < HEAD_DIMENSION


def dot(a, b):
    return jnp.dot(a, b, preferred_element_type=jnp.float32)


def dot_rows(a, b):
    return lax.dot_general(a, b, (((1,), (1,)), ((), ())), preferred_element_type=jnp.float32)


def select(both, rows, columns=slice(0, PAIR)):
    return jnp.where(first_head((rows, PAIR)), both[:rows, columns], both[rows:, columns])


def order_rows_of_pair(sizes, offset, pair, count):
    return jnp.concatenate([order_rows(sizes, offset(2 * pair + n))[:count] for n in range(2)], 0)


def fetch(sources, targets, sems):
    copies = [pltpu.make_async_copy(s, t, sems.at[n]) for n, (s, t) in enumerate(zip(sources, targets))]
    for copy in copies:
        copy.start()
    for copy in copies:
        copy.wait()


def first_kernel(sizes, *refs):
    qd_ref, first_ref, second_ref = refs[4:7]
    off_ref, q_ref, k_ref, v_ref, sems = refs[7:]
    fetch(refs[:4], (off_ref, q_ref, k_ref, v_ref), sems)
    kept, rest, count = sizes.kept_pad, sizes.rest_pad, sizes.all_pad
    scale = HEAD_DIMENSION ** (-0.5)
    for pair in range(q_ref.shape[1] // PAIR):
        cols = slice(pair * PAIR, (pair + 1) * PAIR)
        chosen = order_rows_of_pair(sizes, lambda head: off_ref[head], pair, count)
        both = dot(chosen, jnp.concatenate([q_ref[:, cols], k_ref[:, cols], v_ref[:, cols]], 1))
        q = select(both, count)[:kept] * scale
        k = select(both, count, slice(PAIR, 2 * PAIR)).astype(jnp.bfloat16)
        v = select(both, count, slice(2 * PAIR, 3 * PAIR)).astype(jnp.bfloat16)
        qd_ref[:, cols] = q.astype(jnp.bfloat16)
        first_ref[:kept, cols] = k[:kept]
        first_ref[kept:, cols] = v[:kept]
        second_ref[:rest, cols] = k[kept:]
        second_ref[rest:, cols] = v[kept:]


def order_kernel(sizes, off_ref, q_ref, qs_ref, back_ref, spread_ref):
    width = q_ref.shape[1]
    scale = HEAD_DIMENSION ** (-0.5)
    for pair in range(width // PAIR):
        cols = slice(pair * PAIR, (pair + 1) * PAIR)
        chosen = order_rows_of_pair(sizes, lambda head: off_ref[head], pair, sizes.all_pad)
        qs_ref[:, cols] = (select(dot(chosen, q_ref[:, cols]), sizes.all_pad) * scale).astype(jnp.bfloat16)
        for head in (2 * pair, 2 * pair + 1):
            back_ref[head * sizes.rows : (head + 1) * sizes.rows] = restore_rows(sizes, off_ref[head])
    spread_ref[:, :width] = spread(width, (0,))
    spread_ref[:, width:] = spread(width, (1, 2))


def rows_of(device, begin, count, cols):
    found = []
    for ref, base, size in device:
        low, high = max(begin, 0), min(begin + count, size)
        if low < high:
            found.append(ref[base + low : base + high, cols])
        begin -= size
    return found


def both_heads(q):
    mask = first_head(q.shape)
    zero = jnp.zeros_like(q)
    return jnp.concatenate([jnp.where(mask, q, zero), jnp.where(mask, zero, q)], 0)


def with_ones(v):
    return jnp.concatenate([v, jnp.ones_like(v)], 1)


def hide(col, step, used):
    return jnp.where(lax.rem(col + step, step) < used, 0.0, LOWEST)


def weigh(scores, top, v):
    weights = jnp.exp(scores - top).astype(jnp.bfloat16)
    return dot(weights, with_ones(v))


def whole(ref):
    return [(ref, 0, ref.shape[0])]


def in_turn(sizes, refs):
    found = [[(r, n * sizes.first, sizes.first)] for n in range(sizes.sub) for r in refs]
    return found[: sizes.sub], found[sizes.sub :]


def join(devices, begin, count, cols):
    return [x for d in devices for x in rows_of(d, begin, count, cols)]


def collect_kernel(count, *refs):
    begin = 0
    for r in refs[:count]:
        refs[-1][begin : begin + r.shape[0]] = r[...]
        begin += r.shape[0]


def partial_kernel(sizes, others, q_ref, visitor_ref, lot_ref, other_lot_ref, *out_refs):
    here, beside = in_turn(sizes, (lot_ref, other_lot_ref))
    devices = here + beside
    width = q_ref.shape[1]
    kept = sizes.kept_pad
    rows = (others + 1) * kept
    col = lax.broadcasted_iota(jnp.int32, (2 * rows, 2 * sizes.kept_keys), 1)
    row = lax.broadcasted_iota(jnp.int32, (2 * rows, 2 * sizes.kept_keys), 0)
    row = jnp.where(row < rows, row, row - rows)
    known = jnp.where(row >= others * kept, 1, 0) * jnp.where(col < sizes.kept_keys, 1, 0)
    hidden = jnp.where(known == 1, LOWEST, 0.0)
    if sizes.padded:
        hidden += hide(col, kept, sizes.kept)
    lane = lax.broadcasted_iota(jnp.int32, (rows, PAIR), 1)
    stats = jnp.zeros((rows, PAIR), jnp.float32)
    for pair in range(width // PAIR):
        cols = slice(pair * PAIR, (pair + 1) * PAIR)
        q = jnp.concatenate([visitor_ref[:, cols], q_ref[:kept, cols]], 0)
        k = jnp.concatenate(join(devices, 0, kept, cols), 0)
        v = jnp.concatenate(join(devices, kept, kept, cols), 0)
        scores = dot_rows(both_heads(q), k) + hidden
        top = jnp.max(scores, 1, keepdims=True).astype(jnp.bfloat16).astype(jnp.float32)
        both = weigh(scores, top, v)
        lead, follow = both[:rows], both[rows:]
        out = select(both, rows).astype(jnp.bfloat16)
        for n, r in enumerate(out_refs):
            r[:, cols] = out[n * kept : (n + 1) * kept]
        for n, part in enumerate((lead, follow)):
            head = 3 * (2 * pair + n)
            total = part[:, PAIR:]
            coarse = total.astype(jnp.bfloat16).astype(jnp.float32)
            stats = jnp.where(lane == head, top[n * rows : (n + 1) * rows], stats)
            stats = jnp.where(lane == head + 1, coarse, stats)
            stats = jnp.where(lane == head + 2, total - coarse, stats)
    stats = stats.astype(jnp.bfloat16)
    for n, r in enumerate(out_refs):
        r[:, width:] = stats[n * kept : (n + 1) * kept]


def dense_kernel(sizes, *refs):
    back_ref, q_ref = refs[:2]
    lot_refs, near_refs, far_refs = refs[2:4], refs[4:6], refs[6:-4]
    second = [whole(r) for r in near_refs]
    second += [[(r, core * sizes.second, sizes.second)] for r in far_refs for core in range(2)]
    devices = [d + more for d, more in zip(in_turn(sizes, lot_refs)[0], second)]
    base_ref, out_ref, total_ref, top_ref = refs[-4:]
    width = q_ref.shape[1]
    kept, rest, rows = sizes.kept_pad, sizes.rest_pad, sizes.all_pad
    begin = sizes.kept_keys
    results = []
    for pair in range(width // PAIR):
        cols = slice(pair * PAIR, (pair + 1) * PAIR)
        k = jnp.concatenate(join(devices, 0, kept, cols) + join(devices, 2 * kept, rest, cols), 0)
        v = jnp.concatenate(join(devices, kept, kept, cols) + join(devices, kept + rows, rest, cols), 0)
        scores = dot_rows(both_heads(q_ref[:, cols]), k)
        if sizes.padded:
            col = lax.broadcasted_iota(jnp.int32, (1, sizes.keys), 1)
            here = hide(col, kept, sizes.kept)
            there = hide(col - begin + sizes.keys * rest, rest, sizes.rest)
            scores += jnp.where(col < begin, here, there)
        top = jnp.max(scores, 1, keepdims=True)
        weights = jnp.exp(scores - top)
        near, far = weights[:, :begin], weights[:, begin:]
        near = jnp.concatenate(
            [near[:kept] * 2.0, near[kept:rows], near[rows : rows + kept] * 2.0, near[rows + kept :]], 0
        )
        weights = jnp.concatenate([near, far], 1).astype(jnp.bfloat16)
        both = dot(weights, with_ones(v))
        out, total = select(both, rows), select(both, rows, slice(PAIR, 2 * PAIR))
        out_ref[:, cols], total_ref[:, cols] = out[:kept], total[:kept]
        top_ref[:, cols] = jnp.where(first_head((kept, PAIR)), top[:kept], top[rows : rows + kept])
        results.append((out[kept:] / total[kept:]).astype(jnp.bfloat16))
    for pair, result in enumerate(results):
        cols = slice(pair * PAIR, (pair + 1) * PAIR)
        back = back_ref[2 * sizes.rows * pair : 2 * sizes.rows * (pair + 1)]
        whole_rows = jnp.concatenate([jnp.zeros((kept, PAIR), jnp.bfloat16), result], 0)
        base_ref[:, cols] = select(dot(back, whole_rows), sizes.rows).astype(jnp.bfloat16)


def dense_shapes(sizes, width):
    shapes = [(sizes.rows, width, jnp.bfloat16)]
    shapes += [(sizes.kept_pad, width, jnp.float32)] * 3
    return [jax.ShapeDtypeStruct(s[:2], s[2]) for s in shapes]


def spread(width, lanes):
    lane = lax.broadcasted_iota(jnp.int32, (PAIR, width), 0)
    head = jnp.right_shift(lax.broadcasted_iota(jnp.int32, (PAIR, width), 1), HEAD_DIMENSION.bit_length() - 1)
    hits = [jnp.where(lane == 3 * head + n, 1.0, 0.0) for n in lanes]
    return sum(hits).astype(jnp.bfloat16)


def merge_kernel(sizes, *refs):
    back_ref, spread_ref, base_ref, out_ref, total_ref, top_ref = refs[:6]
    part_refs, done_hbm, done_ref, sems = refs[6:-3], refs[-3], refs[-2], refs[-1]
    others = len(part_refs)
    width = out_ref.shape[1]
    kept = sizes.kept_pad
    stats = jnp.concatenate([r[:, width:] for r in part_refs], 0)
    tops = dot(stats, spread_ref[:, :width])
    totals = dot(stats, spread_ref[:, width:])
    theirs = [tops[n * kept : (n + 1) * kept] for n in range(others)]
    top = top_ref[...]
    best = functools.reduce(jnp.maximum, theirs, top)
    factor = jnp.exp(top - best)
    out, total = out_ref[...] * factor, total_ref[...] * factor
    for n, r in enumerate(part_refs):
        factor = jnp.exp(theirs[n] - best)
        out += r[:, :width].astype(jnp.float32) * factor
        total += totals[n * kept : (n + 1) * kept] * factor
    result = (out / total).astype(jnp.bfloat16)
    leaving, half = [], width // 2
    for pair in range(width // PAIR):
        cols = slice(pair * PAIR, (pair + 1) * PAIR)
        back = dot(back_ref[2 * sizes.rows * pair : 2 * sizes.rows * (pair + 1), :kept], result[:, cols])
        done_ref[:, cols] = (select(back, sizes.rows) + base_ref[:, cols].astype(jnp.float32)).astype(jnp.bfloat16)
        if (pair + 1) * PAIR in (half, width):
            part = pl.ds(half * len(leaving), half)
            copy = pltpu.make_async_copy(done_ref.at[:, part], done_hbm.at[:, part], sems.at[len(leaving)])
            copy.start()
            leaving.append(copy)
    for copy in leaving:
        copy.wait()


def call(kernel, out_shape, operands, flops, place=pltpu.VMEM, scratch=(), limit=24, out_place=pltpu.VMEM):
    spec = pl.BlockSpec(memory_space=place)
    smem = pl.BlockSpec(memory_space=pltpu.SMEM)
    in_specs = [smem if x.ndim == 1 and place == pltpu.VMEM else spec for x in operands]
    out_specs = jax.tree.map(lambda _: pl.BlockSpec(memory_space=out_place), out_shape)
    size = sum(x.size * 2 for x in operands)
    return pl.pallas_call(
        kernel,
        out_shape=out_shape,
        in_specs=in_specs,
        out_specs=out_specs,
        scratch_shapes=scratch,
        cost_estimate=pl.CostEstimate(flops=flops, bytes_accessed=size, transcendentals=0),
        compiler_params=pltpu.CompilerParams(vmem_limit_bytes=int(limit * 1024 * 1024)),
    )(*operands)


def per_device(queries, keys, values, offsets):
    rows, width = queries.shape
    seq, sub = lax.axis_size("seq"), lax.axis_size("sub")
    sizes = Sizes(rows, seq, sub)

    def array(count, columns=width, dtype=jnp.bfloat16):
        return jax.ShapeDtypeStruct((count, columns), dtype)

    def swap(x, axis, mask):
        return lax.ppermute(x, axis, [(n, n ^ mask) for n in range(lax.axis_size(axis))])

    def after(x, *earlier):
        return lax.optimization_barrier((x, *earlier))[0]

    def far(x):
        return [swap(x, "sub", mask) for mask in range(2, sub, 2)]

    def both_cores(lines):
        chips = [[n, n + 1] for n in range(0, sub, 2)]
        return [lax.all_gather(x, "sub", axis=0, tiled=True, axis_index_groups=chips) for x in lines]

    def swap_both(x, mask):
        size = seq * sub
        return lax.ppermute(x, ("seq", "sub"), [(n, n ^ sub ^ mask) for n in range(size)])

    masks, far_masks = range(2, seq, 2), range(2, sub, 2)
    heads = width // HEAD_DIMENSION
    q_kept, first, second = call(
        functools.partial(first_kernel, sizes),
        [array(n) for n in (sizes.kept_pad, sizes.first, sizes.second)],
        (offsets, queries, keys, values),
        COST[0],
        pltpu.HBM,
        [pltpu.SMEM(offsets.shape, jnp.int32)]
        + [pltpu.VMEM((rows, width), jnp.bfloat16)] * 3
        + [pltpu.SemaphoreType.DMA((4,))],
        LIMIT,
    )
    far_first = far(first)
    lot = [first] + far_first + [swap(first, "seq", 1)] + [swap_both(first, mask) for mask in far_masks]
    far_second = far(second)
    q, back, spreads = call(
        functools.partial(order_kernel, sizes),
        [array(sizes.all_pad), array(heads * rows, sizes.all_pad), array(PAIR, 2 * width)],
        (offsets, queries),
        COST[1],
    )
    visitors = [swap(q_kept, "seq", mask) for mask in masks]
    lot = call(
        functools.partial(collect_kernel, len(lot)), array(len(lot) * sizes.first), (*lot, q), COST[2]
    )
    near_second = [second, swap(after(second, lot), "sub", 1)]
    lot = [lot, swap(lot, "sub", 1)]
    visitors = call(
        functools.partial(collect_kernel, len(masks)),
        array(len(masks) * sizes.kept_pad),
        visitors,
        COST[3],
    )
    *parts, own_part = call(
        functools.partial(partial_kernel, sizes, len(masks)),
        [array(sizes.kept_pad, width + PAIR)] * (len(masks) + 1),
        (q, visitors, *lot),
        COST[5],
    )
    returned = [swap(part, "seq", mask) for mask, part in zip(masks, parts)]
    far_second = both_cores([after(x, *parts) for x in far_second])
    dense = call(
        functools.partial(dense_kernel, sizes),
        dense_shapes(sizes, width),
        (back, q, *lot, *near_second, *far_second),
        COST[6],
    )
    return call(
        functools.partial(merge_kernel, sizes),
        array(rows),
        (back, spreads, *dense, *returned, own_part),
        COST[7],
        scratch=[pltpu.VMEM((rows, width), jnp.bfloat16), pltpu.SemaphoreType.DMA((2,))],
        out_place=pltpu.HBM,
    )


def solution(mesh):
    placed = P(("rep", "seq", "sub"), None)
    return jax.shard_map(
        per_device,
        mesh=mesh,
        in_specs=(placed, placed, placed, P()),
        out_specs=placed,
        check_vma=False,
    )
```

```python
import functools

import jax
import jax.numpy as jnp
from jax import lax
from jax.experimental import pallas as pl
from jax.experimental.pallas import tpu as pltpu
from jax.sharding import PartitionSpec as P

ATTENTION_HEADS = 12
HEAD_DIMENSION = 64
PAIR = 2 * HEAD_DIMENSION
LOWEST = -1e30
LIMIT = 56
COST = (10**6, 10**6, 10**10, 10**10, 0, 10**6, 10**6, 10**6)


def round_up(count, step):
    return -(-count // step) * step


class Sizes:
    def __init__(self, rows, dilation, sub):
        self.rows, self.dilation, self.sub = rows, dilation, sub
        self.kept = rows // dilation
        self.rest = rows - self.kept
        self.kept_pad = round_up(self.kept, 16)
        self.rest_pad = round_up(self.rest, 16)
        self.all_pad = self.kept_pad + self.rest_pad
        self.first = 2 * self.kept_pad
        self.second = 2 * self.rest_pad
        self.shift = dilation.bit_length() - 1
        self.kept_keys = sub * self.kept_pad
        self.keys = sub * self.all_pad
        self.padded = self.kept_pad != self.kept or self.rest_pad != self.rest


def target_rows(sizes, position, offset):
    residue = jnp.bitwise_and(position, sizes.dilation - 1)
    group = jnp.right_shift(position, sizes.shift)
    slab = jnp.bitwise_and(residue - offset + sizes.dilation, sizes.dilation - 1)
    return jnp.where(slab == 0, group, sizes.kept_pad + (slab - 1) * sizes.kept + group)


def order_rows(sizes, offset):
    shape = (sizes.all_pad, sizes.rows)
    place = lax.broadcasted_iota(jnp.int32, shape, 0)
    target = target_rows(sizes, lax.broadcasted_iota(jnp.int32, (1, sizes.rows), 1), offset)
    return jnp.where(place == target, 1.0, 0.0).astype(jnp.bfloat16)


def restore_rows(sizes, offset):
    shape = (sizes.rows, sizes.all_pad)
    place = lax.broadcasted_iota(jnp.int32, shape, 1)
    target = target_rows(sizes, lax.broadcasted_iota(jnp.int32, shape, 0), offset)
    return jnp.where(place == target, 1.0, 0.0).astype(jnp.bfloat16)


def first_head(shape):
    return lax.broadcasted_iota(jnp.int32, shape, 1) < HEAD_DIMENSION


def dot(a, b):
    return jnp.dot(a, b, preferred_element_type=jnp.float32)


def dot_rows(a, b):
    return lax.dot_general(a, b, (((1,), (1,)), ((), ())), preferred_element_type=jnp.float32)


def select(both, rows, columns=slice(0, PAIR)):
    return jnp.where(first_head((rows, PAIR)), both[:rows, columns], both[rows:, columns])


def order_rows_of_pair(sizes, offset, pair, count):
    return jnp.concatenate([order_rows(sizes, offset(2 * pair + n))[:count] for n in range(2)], 0)


def fetch(sources, targets, sems):
    copies = [pltpu.make_async_copy(s, t, sems.at[n]) for n, (s, t) in enumerate(zip(sources, targets))]
    for copy in copies:
        copy.start()
    for copy in copies:
        copy.wait()


def first_kernel(sizes, *refs):
    qd_ref, first_ref, second_ref = refs[4:7]
    off_ref, q_ref, k_ref, v_ref, sems = refs[7:]
    fetch(refs[:4], (off_ref, q_ref, k_ref, v_ref), sems)
    kept, rest, count = sizes.kept_pad, sizes.rest_pad, sizes.all_pad
    scale = HEAD_DIMENSION ** (-0.5)
    for pair in range(q_ref.shape[1] // PAIR):
        cols = slice(pair * PAIR, (pair + 1) * PAIR)
        chosen = order_rows_of_pair(sizes, lambda head: off_ref[head], pair, count)
        both = dot(chosen, jnp.concatenate([q_ref[:, cols], k_ref[:, cols], v_ref[:, cols]], 1))
        q = select(both, count)[:kept] * scale
        k = select(both, count, slice(PAIR, 2 * PAIR)).astype(jnp.bfloat16)
        v = select(both, count, slice(2 * PAIR, 3 * PAIR)).astype(jnp.bfloat16)
        qd_ref[:, cols] = q.astype(jnp.bfloat16)
        first_ref[:kept, cols] = k[:kept]
        first_ref[kept:, cols] = v[:kept]
        second_ref[:rest, cols] = k[kept:]
        second_ref[rest:, cols] = v[kept:]


def order_kernel(sizes, off_ref, q_ref, k_ref, v_ref, qs_ref, back_ref, spread_ref, near_ref):
    width = q_ref.shape[1]
    scale = HEAD_DIMENSION ** (-0.5)
    for pair in range(width // PAIR):
        cols = slice(pair * PAIR, (pair + 1) * PAIR)
        chosen = order_rows_of_pair(sizes, lambda head: off_ref[head], pair, sizes.all_pad)
        both = dot(chosen, jnp.concatenate([r[:, cols] for r in (q_ref, k_ref, v_ref)], 1))
        qs_ref[:, cols] = (select(both, sizes.all_pad) * scale).astype(jnp.bfloat16)
        for n in (1, 2):
            found = select(both, sizes.all_pad, slice(n * PAIR, (n + 1) * PAIR))[sizes.kept_pad :]
            near_ref[(n - 1) * sizes.rest_pad : n * sizes.rest_pad, cols] = found.astype(jnp.bfloat16)
        for head in (2 * pair, 2 * pair + 1):
            back_ref[head * sizes.rows : (head + 1) * sizes.rows] = restore_rows(sizes, off_ref[head])
    spread_ref[:, :width] = spread(width, (0,))
    spread_ref[:, width:] = spread(width, (1, 2))


def rows_of(device, begin, count, cols):
    found = []
    for ref, base, size in device:
        low, high = max(begin, 0), min(begin + count, size)
        if low < high:
            found.append(ref[base + low : base + high, cols])
        begin -= size
    return found


def both_heads(q):
    mask = first_head(q.shape)
    zero = jnp.zeros_like(q)
    return jnp.concatenate([jnp.where(mask, q, zero), jnp.where(mask, zero, q)], 0)


def with_ones(v):
    return jnp.concatenate([v, jnp.ones_like(v)], 1)


def hide(col, step, used):
    return jnp.where(lax.rem(col + step, step) < used, 0.0, LOWEST)


def weigh(scores, top, v):
    weights = jnp.exp(scores - top).astype(jnp.bfloat16)
    return dot(weights, with_ones(v))


def whole(ref):
    return [(ref, 0, ref.shape[0])]


def in_turn(sizes, refs):
    found = [[(r, n * sizes.first, sizes.first)] for n in range(sizes.sub) for r in refs]
    return found[: sizes.sub], found[sizes.sub :]


def join(devices, begin, count, cols):
    return [x for d in devices for x in rows_of(d, begin, count, cols)]


def collect_kernel(count, *refs):
    begin = 0
    for r in refs[:count]:
        refs[-1][begin : begin + r.shape[0]] = r[...]
        begin += r.shape[0]


def partial_kernel(sizes, others, q_ref, visitor_ref, lot_ref, other_lot_ref, *out_refs):
    here, beside = in_turn(sizes, (lot_ref, other_lot_ref))
    devices = here + beside
    width = q_ref.shape[1]
    kept = sizes.kept_pad
    rows = (others + 1) * kept
    col = lax.broadcasted_iota(jnp.int32, (2 * rows, 2 * sizes.kept_keys), 1)
    row = lax.broadcasted_iota(jnp.int32, (2 * rows, 2 * sizes.kept_keys), 0)
    row = jnp.where(row < rows, row, row - rows)
    known = jnp.where(row >= others * kept, 1, 0) * jnp.where(col < sizes.kept_keys, 1, 0)
    hidden = jnp.where(known == 1, LOWEST, 0.0)
    if sizes.padded:
        hidden += hide(col, kept, sizes.kept)
    lane = lax.broadcasted_iota(jnp.int32, (rows, PAIR), 1)
    stats = jnp.zeros((rows, PAIR), jnp.float32)
    for pair in range(width // PAIR):
        cols = slice(pair * PAIR, (pair + 1) * PAIR)
        q = jnp.concatenate([visitor_ref[:, cols], q_ref[:kept, cols]], 0)
        k = jnp.concatenate(join(devices, 0, kept, cols), 0)
        v = jnp.concatenate(join(devices, kept, kept, cols), 0)
        scores = dot_rows(both_heads(q), k) + hidden
        top = jnp.max(scores, 1, keepdims=True).astype(jnp.bfloat16).astype(jnp.float32)
        both = weigh(scores, top, v)
        lead, follow = both[:rows], both[rows:]
        out = select(both, rows).astype(jnp.bfloat16)
        for n, r in enumerate(out_refs):
            r[:, cols] = out[n * kept : (n + 1) * kept]
        for n, part in enumerate((lead, follow)):
            head = 3 * (2 * pair + n)
            total = part[:, PAIR:]
            coarse = total.astype(jnp.bfloat16).astype(jnp.float32)
            stats = jnp.where(lane == head, top[n * rows : (n + 1) * rows], stats)
            stats = jnp.where(lane == head + 1, coarse, stats)
            stats = jnp.where(lane == head + 2, total - coarse, stats)
    stats = stats.astype(jnp.bfloat16)
    for n, r in enumerate(out_refs):
        r[:, width:] = stats[n * kept : (n + 1) * kept]


def dense_kernel(sizes, *refs):
    back_ref, q_ref = refs[:2]
    lot_refs, near_refs, far_refs = refs[2:4], refs[4:6], refs[6:-4]
    second = [whole(r) for r in near_refs]
    second += [[(r, core * sizes.second, sizes.second)] for r in far_refs for core in range(2)]
    devices = [d + more for d, more in zip(in_turn(sizes, lot_refs)[0], second)]
    base_ref, out_ref, total_ref, top_ref = refs[-4:]
    width = q_ref.shape[1]
    kept, rest, rows = sizes.kept_pad, sizes.rest_pad, sizes.all_pad
    begin = sizes.kept_keys
    results = []
    for pair in range(width // PAIR):
        cols = slice(pair * PAIR, (pair + 1) * PAIR)
        k = jnp.concatenate(join(devices, 0, kept, cols) + join(devices, 2 * kept, rest, cols), 0)
        v = jnp.concatenate(join(devices, kept, kept, cols) + join(devices, kept + rows, rest, cols), 0)
        scores = dot_rows(both_heads(q_ref[:, cols]), k)
        if sizes.padded:
            col = lax.broadcasted_iota(jnp.int32, (1, sizes.keys), 1)
            here = hide(col, kept, sizes.kept)
            there = hide(col - begin + sizes.keys * rest, rest, sizes.rest)
            scores += jnp.where(col < begin, here, there)
        top = jnp.max(scores, 1, keepdims=True)
        weights = jnp.exp(scores - top)
        near, far = weights[:, :begin], weights[:, begin:]
        near = jnp.concatenate(
            [near[:kept] * 2.0, near[kept:rows], near[rows : rows + kept] * 2.0, near[rows + kept :]], 0
        )
        weights = jnp.concatenate([near, far], 1).astype(jnp.bfloat16)
        both = dot(weights, with_ones(v))
        out, total = select(both, rows), select(both, rows, slice(PAIR, 2 * PAIR))
        out_ref[:, cols], total_ref[:, cols] = out[:kept], total[:kept]
        top_ref[:, cols] = jnp.where(first_head((kept, PAIR)), top[:kept], top[rows : rows + kept])
        results.append((out[kept:] / total[kept:]).astype(jnp.bfloat16))
    for pair, result in enumerate(results):
        cols = slice(pair * PAIR, (pair + 1) * PAIR)
        back = back_ref[2 * sizes.rows * pair : 2 * sizes.rows * (pair + 1)]
        whole_rows = jnp.concatenate([jnp.zeros((kept, PAIR), jnp.bfloat16), result], 0)
        base_ref[:, cols] = select(dot(back, whole_rows), sizes.rows).astype(jnp.bfloat16)


def dense_shapes(sizes, width):
    shapes = [(sizes.rows, width, jnp.bfloat16)]
    shapes += [(sizes.kept_pad, width, jnp.float32)] * 3
    return [jax.ShapeDtypeStruct(s[:2], s[2]) for s in shapes]


def spread(width, lanes):
    lane = lax.broadcasted_iota(jnp.int32, (PAIR, width), 0)
    head = jnp.right_shift(lax.broadcasted_iota(jnp.int32, (PAIR, width), 1), HEAD_DIMENSION.bit_length() - 1)
    hits = [jnp.where(lane == 3 * head + n, 1.0, 0.0) for n in lanes]
    return sum(hits).astype(jnp.bfloat16)


def merge_kernel(sizes, *refs):
    back_ref, spread_ref, base_ref, out_ref, total_ref, top_ref = refs[:6]
    part_refs, done_ref = refs[6:-1], refs[-1]
    others = len(part_refs)
    width = out_ref.shape[1]
    kept = sizes.kept_pad
    stats = jnp.concatenate([r[:, width:] for r in part_refs], 0)
    tops = dot(stats, spread_ref[:, :width])
    totals = dot(stats, spread_ref[:, width:])
    theirs = [tops[n * kept : (n + 1) * kept] for n in range(others)]
    top = top_ref[...]
    best = functools.reduce(jnp.maximum, theirs, top)
    factor = jnp.exp(top - best)
    out, total = out_ref[...] * factor, total_ref[...] * factor
    for n, r in enumerate(part_refs):
        factor = jnp.exp(theirs[n] - best)
        out += r[:, :width].astype(jnp.float32) * factor
        total += totals[n * kept : (n + 1) * kept] * factor
    result = (out / total).astype(jnp.bfloat16)
    for pair in range(width // PAIR):
        cols = slice(pair * PAIR, (pair + 1) * PAIR)
        back = dot(back_ref[2 * sizes.rows * pair : 2 * sizes.rows * (pair + 1), :kept], result[:, cols])
        done_ref[:, cols] = (select(back, sizes.rows) + base_ref[:, cols].astype(jnp.float32)).astype(jnp.bfloat16)


def call(kernel, out_shape, operands, flops, place=pltpu.VMEM, scratch=(), limit=24):
    spec = pl.BlockSpec(memory_space=place)
    smem = pl.BlockSpec(memory_space=pltpu.SMEM)
    in_specs = [smem if x.ndim == 1 and place == pltpu.VMEM else spec for x in operands]
    out_specs = jax.tree.map(lambda _: pl.BlockSpec(memory_space=pltpu.VMEM), out_shape)
    size = sum(x.size * 2 for x in operands)
    return pl.pallas_call(
        kernel,
        out_shape=out_shape,
        in_specs=in_specs,
        out_specs=out_specs,
        scratch_shapes=scratch,
        cost_estimate=pl.CostEstimate(flops=flops, bytes_accessed=size, transcendentals=0),
        compiler_params=pltpu.CompilerParams(vmem_limit_bytes=int(limit * 1024 * 1024)),
    )(*operands)


def per_device(queries, keys, values, offsets):
    rows, width = queries.shape
    seq, sub = lax.axis_size("seq"), lax.axis_size("sub")
    sizes = Sizes(rows, seq, sub)

    def array(count, columns=width, dtype=jnp.bfloat16):
        return jax.ShapeDtypeStruct((count, columns), dtype)

    def swap(x, axis, mask):
        return lax.ppermute(x, axis, [(n, n ^ mask) for n in range(lax.axis_size(axis))])

    def after(x, *earlier):
        return lax.optimization_barrier((x, *earlier))[0]

    def far(x):
        return [swap(x, "sub", mask) for mask in range(2, sub, 2)]

    def both_cores(lines):
        chips = [[n, n + 1] for n in range(0, sub, 2)]
        return [lax.all_gather(x, "sub", axis=0, tiled=True, axis_index_groups=chips) for x in lines]

    def swap_both(x, mask):
        size = seq * sub
        return lax.ppermute(x, ("seq", "sub"), [(n, n ^ sub ^ mask) for n in range(size)])

    masks, far_masks = range(2, seq, 2), range(2, sub, 2)
    heads = width // HEAD_DIMENSION
    q_kept, first, second = call(
        functools.partial(first_kernel, sizes),
        [array(n) for n in (sizes.kept_pad, sizes.first, sizes.second)],
        (offsets, queries, keys, values),
        COST[0],
        pltpu.HBM,
        [pltpu.SMEM(offsets.shape, jnp.int32)]
        + [pltpu.VMEM((rows, width), jnp.bfloat16)] * 3
        + [pltpu.SemaphoreType.DMA((4,))],
        LIMIT,
    )
    far_first = far(first)
    lot = [first] + far_first + [swap(first, "seq", 1)] + [swap_both(first, mask) for mask in far_masks]
    far_second = far(second)
    q, back, spreads, near = call(
        functools.partial(order_kernel, sizes),
        [array(sizes.all_pad), array(heads * rows, sizes.all_pad), array(PAIR, 2 * width), array(sizes.second)],
        (offsets, queries, keys, values),
        COST[1],
    )
    visitors = [swap(q_kept, "seq", mask) for mask in masks]
    lot = call(
        functools.partial(collect_kernel, len(lot)), array(len(lot) * sizes.first), (*lot, q), COST[2]
    )
    near_second = [near, swap(after(near, lot), "sub", 1)]
    lot = [lot, swap(lot, "sub", 1)]
    visitors = call(
        functools.partial(collect_kernel, len(masks)),
        array(len(masks) * sizes.kept_pad),
        visitors,
        COST[3],
    )
    *parts, own_part = call(
        functools.partial(partial_kernel, sizes, len(masks)),
        [array(sizes.kept_pad, width + PAIR)] * (len(masks) + 1),
        (q, visitors, *lot),
        COST[5],
    )
    returned = [swap(part, "seq", mask) for mask, part in zip(masks, parts)]
    far_second = both_cores([after(x, *parts) for x in far_second])
    dense = call(
        functools.partial(dense_kernel, sizes),
        dense_shapes(sizes, width),
        (back, q, *lot, *near_second, *far_second),
        COST[6],
    )
    return call(functools.partial(merge_kernel, sizes), array(rows), (back, spreads, *dense, *returned, own_part), COST[7])


def solution(mesh):
    placed = P(("rep", "seq", "sub"), None)
    return jax.shard_map(
        per_device,
        mesh=mesh,
        in_specs=(placed, placed, placed, P()),
        out_specs=placed,
        check_vma=False,
    )
```
